128 devices in a mesh: dp: 8 (over z, y_lo), fsdp: 16 (over y_hi, x, core).
Axes of the slice: x: 4, y: 4 (y_hi: 2, y_lo: 2; y = y_hi * 2 + y_lo), z: 4, core: 2. Of those that a mesh axis runs over, the one named last changes fastest.
Arguments:
- tokens: bfloat16 [4096, 3072], P('fsdp'), may hold values from -6 to 6
- cotangent: bfloat16 [4096, 3072], P('fsdp'), may hold values from -6 to 6
- w_in: bfloat16 [3072, 12288], P('fsdp', 'dp'), may hold values from -0.4690971 to 0.4690971
- w_out: bfloat16 [12288, 3072], P('dp', 'fsdp'), may hold values from -0.23454855 to 0.23454855
Outputs:
- grad_in: float32 [3072, 12288], P('fsdp', 'dp')
- grad_out: float32 [12288, 3072], P('dp', 'fsdp')
- input_grad: bfloat16 [4096, 3072], P('fsdp')
The draws below stay inside these ranges and needn't reach their ends.
All inputs are finite; a program needn't handle non-finite values.
Results may differ from the reference program's by a relative error of at most 0.019.
Values may be sent and summed in bfloat16 or wider, within the bound.
A program may use at most 192 MiB of HBM per device.

```python
import math
import jax
import jax.numpy as jnp
from jax import lax

D = 3072
FF = 12288
TOK_DEV = 256
TOKENS = 4096
N_FSDP = 16


def spread_gains(key_gain, amount, growth):
    position = jnp.arange(amount, dtype=jnp.float32) / amount
    exponent = jax.random.uniform(key_gain, (amount,), jnp.float32)
    return 10.0 ** exponent * growth ** position / 6.0


def draw_w_in(key, part):
    key = jax.random.fold_in(key, 11)
    key_gain, key_entries = jax.random.split(key)
    column_gain = spread_gains(key_gain, FF, 3.0)
    entries = jax.random.truncated_normal(key_entries, -4.0, 4.0, (D, FF), jnp.float32)
    return (entries * column_gain[None, :] / math.sqrt(D)).astype(jnp.bfloat16)


def draw_w_out(key, part):
    key = jax.random.fold_in(key, 12)
    key_gain, key_entries = jax.random.split(key)
    row_gain = spread_gains(key_gain, FF, 3.0)
    entries = jax.random.truncated_normal(key_entries, -4.0, 4.0, (FF, D), jnp.float32)
    return (entries * row_gain[:, None] / math.sqrt(FF)).astype(jnp.bfloat16)


def with_spikes(result, own_key, source, target, parts, factor):
    owner, partner = [(jnp.arange(result.shape[axis_at]) // (result.shape[axis_at] // parts)).reshape([-1 if axis == axis_at else 1 for axis in range(result.ndim)]) for axis_at in (source, target)]
    chosen = jax.random.permutation(own_key, parts)[partner]
    strong = (owner == chosen) | (owner == (partner + parts // 2) % parts)
    return jnp.where(strong, factor * result, result)


def block_scale(stream_key, dims, shards, low, top_value):
    def one(axis_at, blocks):
        draws = jax.random.uniform(jax.random.fold_in(jax.random.fold_in(stream_key, 6), axis_at), (blocks,), jnp.float32, low / len(shards), top_value / len(shards))
        return jnp.repeat(jnp.exp(draws), dims[axis_at] // blocks).reshape((-1,) + (1,) * (len(dims) - axis_at - 1))

    factor_of = one(*shards[0])
    for cut in shards[1:]:
        factor_of = factor_of * one(*cut)
    return factor_of


def heavy_noise(rng, dims, spread, bound, shards, heavy, held_as=jnp.bfloat16):
    drawn = spread * jax.random.normal(rng, dims, jnp.float32)
    if shards:
        drawn = drawn * block_scale(rng, dims, shards, -0.22, 0.18)
    return jnp.clip(with_spikes(drawn, jax.random.fold_in(rng, 3), *heavy), -bound, bound).astype(held_as)


def setup_inputs(seed: int = 0) -> dict:
    streams_of = jax.random.split(jax.random.key(seed), 5)
    tokens = heavy_noise(streams_of[0], (TOKENS, D), 1.0, 6.0, ((0, 16),), (0, 1, 16, 2.0))
    cotangent = heavy_noise(streams_of[1], (TOKENS, D), 1.0, 6.0, ((0, 16),), (0, 1, 16, 2.0))
    w_in = draw_w_in(jax.random.fold_in(streams_of[4], 71), 0)
    w_out = draw_w_out(jax.random.fold_in(streams_of[4], 71), 0)
    return {"tokens": tokens, "cotangent": cotangent, "w_in": w_in, "w_out": w_out}


RADIUS_SHARE = 0.5
EPSILON = 1e-06

def gelu_exact(values):
    return jax.nn.gelu(values, approximate=False)

def contract_rows(first_op, second_op):
    return lax.dot_general(first_op, second_op, (((0,), (0,)), ((), ())), preferred_element_type=jnp.float32)

def contract_cols(first_op, second_op):
    return lax.dot_general(first_op, second_op, (((1,), (1,)), ((), ())), preferred_element_type=jnp.float32)

def group_pass(tok_group, cot_group, weight_in, weight_out):
    hidden = jnp.dot(tok_group, weight_in, preferred_element_type=jnp.float32)
    active, pullback = jax.vjp(gelu_exact, hidden)
    back_proj = contract_cols(cot_group, weight_out)
    slope_bf = pullback(back_proj)[0].astype(jnp.bfloat16)
    active_bf = active.astype(jnp.bfloat16)
    return (slope_bf, contract_rows(tok_group, slope_bf), contract_rows(active_bf, cot_group))

def reference(tokens, cotangent, w_in, w_out):
    radius = RADIUS_SHARE * math.sqrt(D + FF)
    grad_scale = 1.0 / math.sqrt(TOKENS)
    token_groups = tokens.reshape(N_FSDP, TOK_DEV, D)
    cot_groups = cotangent.reshape(N_FSDP, TOK_DEV, D)

    def one_group(carry, group):
        sum_in, sum_out = carry
        tok_group, cot_group = group
        unused, ascent_in, ascent_out = group_pass(tok_group, cot_group, w_in, w_out)
        norm_value = jnp.sqrt(jnp.sum(ascent_in * ascent_in) + jnp.sum(ascent_out * ascent_out) + EPSILON)
        factor = radius / norm_value
        moved_in = (w_in.astype(jnp.float32) + factor * ascent_in).astype(jnp.bfloat16)
        moved_out = (w_out.astype(jnp.float32) + factor * ascent_out).astype(jnp.bfloat16)
        slope_two, term_in, term_out = group_pass(tok_group, cot_group, moved_in, moved_out)
        input_rows = contract_cols(slope_two, moved_in).astype(jnp.bfloat16)
        term_in = lax.optimization_barrier(term_in.astype(jnp.bfloat16)).astype(jnp.float32)
        term_out = lax.optimization_barrier(term_out.astype(jnp.bfloat16)).astype(jnp.float32)
        return ((sum_in + term_in, sum_out + term_out), input_rows)
    start_sums = (jnp.zeros((D, FF), jnp.float32), jnp.zeros((FF, D), jnp.float32))
    (sum_in, sum_out), input_rows = lax.scan(one_group, start_sums, (token_groups, cot_groups))
    return (sum_in * grad_scale, sum_out * grad_scale, input_rows.reshape(TOKENS, D))
```

```python
import math

import jax
import jax.numpy as jnp
from jax import lax
from jax.sharding import Mesh, PartitionSpec as P

D = 3072
FF = 12288
GROUP = 256

RADIUS_SHARE = 0.5
EPSILON = 1e-06
AXES = ("z", "ylo", "yhi", "x", "core")
QUAD = ("yhi", "core")
PLANE = ("z", "ylo", "yhi", "core")


def dot(a, b, dims):
    return lax.dot_general(a, b, (dims, ((), ())), preferred_element_type=jnp.float32)


def gelu_pair(h):
    cdf = 0.5 * (1.0 + lax.erf(h * (1.0 / math.sqrt(2.0))))
    pdf = jnp.exp(-0.5 * h * h) * (1.0 / math.sqrt(2.0 * math.pi))
    return h * cdf, cdf + h * pdf


def gram_apply(x, s):
    g = x.shape[0] // GROUP
    x3, s3 = x.reshape(g, GROUP, -1), s.reshape(g, GROUP, -1)
    gram = jnp.einsum("gtd,gud->gtu", x3, x3, preferred_element_type=jnp.float32)
    hi = gram.astype(jnp.bfloat16)
    lo = (gram - hi.astype(jnp.float32)).astype(jnp.bfloat16)
    mm = lambda m: jnp.einsum("gtu,guh->gth", m, s3, preferred_element_type=jnp.float32)
    return mm(hi) + mm(lo)


def on_device(tokens, cotangent, w_in, w_out):
    radius = RADIUS_SHARE * math.sqrt(D + FF)
    grad_scale = 1.0 / math.sqrt(4096)
    tok = lax.all_gather(tokens, QUAD, axis=0, tiled=True)
    cot = lax.all_gather(cotangent, QUAD, axis=0, tiled=True)
    both = jnp.stack([w_in, w_out.T])
    n = both.shape[1]
    quarter = both.shape[2] // 4
    mine = both.reshape(2, n, 4, quarter).transpose(2, 0, 1, 3)
    mine = lax.all_to_all(mine, QUAD, 0, 0)
    full = lax.all_gather(mine, "x", axis=0)
    full = full.reshape(4, 2, 2, 2, n, quarter).transpose(3, 1, 0, 2, 4, 5).reshape(2, D, quarter)
    full_in, full_out = full[0], full[1]
    hidden = dot(tok, full_in, ((1,), (0,)))
    back = dot(cot, full_out, ((1,), (0,)))
    act, der = gelu_pair(hidden)
    act1 = act.astype(jnp.bfloat16)
    slope1 = (back * der).astype(jnp.bfloat16)
    gs = gram_apply(tok, slope1)
    ga = gram_apply(cot, act1)
    g = gs.shape[0]
    square = jnp.sum(gs * slope1.reshape(gs.shape).astype(jnp.float32), axis=(1, 2)) + jnp.sum(
        ga * act1.reshape(ga.shape).astype(jnp.float32), axis=(1, 2)
    )
    square = lax.psum(square, PLANE)
    factor = (radius / jnp.sqrt(square + EPSILON))[:, None, None]
    hidden = hidden + (factor * gs).reshape(hidden.shape)
    back = back + (factor * ga).reshape(hidden.shape)
    act, der = gelu_pair(hidden)
    act2 = act.astype(jnp.bfloat16)
    slope2 = (back * der).astype(jnp.bfloat16)
    cross = jnp.einsum(
        "gth,guh->gtu", slope2.reshape(g, GROUP, -1), slope1.reshape(g, GROUP, -1), preferred_element_type=jnp.float32
    )
    cross = (factor * cross).astype(jnp.bfloat16)
    moved = jnp.einsum("gtu,gud->gtd", cross, tok.reshape(g, GROUP, D), preferred_element_type=jnp.float32)
    partial = dot(slope2, full_in, ((1,), (1,))) + moved.reshape(tok.shape)
    share = lax.psum_scatter(partial.astype(jnp.bfloat16), QUAD, scatter_dimension=0, tiled=True)
    input_grad = lax.psum(share, ("z", "ylo"))
    terms = jnp.stack([dot(tok, slope2, ((0,), (0,))), dot(cot, act2, ((0,), (0,)))]).astype(jnp.bfloat16)
    terms = terms.reshape(2, 2, 4, 2, n, quarter).transpose(2, 1, 3, 0, 4, 5)
    sums = lax.psum_scatter(terms.reshape(-1, quarter), "x", scatter_dimension=0, tiled=True)
    sums = lax.all_to_all(sums.reshape(4, 2, n, quarter), QUAD, 0, 0)
    sums = sums.transpose(1, 2, 0, 3).reshape(2, n, 4 * quarter).astype(jnp.float32) * grad_scale
    return sums[0], sums[1].T, input_grad


def solution(mesh):
    view = Mesh(mesh.devices.reshape(4, 2, 2, 4, 2), AXES)
    fsdp, dp = ("yhi", "x", "core"), ("z", "ylo")
    return jax.shard_map(
        on_device,
        mesh=view,
        in_specs=(P(fsdp, None), P(fsdp, None), P(fsdp, dp), P(dp, fsdp)),
        out_specs=(P(fsdp, dp), P(dp, fsdp), P(fsdp, None)),
        check_vma=False,
    )
```

```python
import math

import jax
import jax.numpy as jnp
from jax import lax
from jax.experimental import pallas as pl
from jax.experimental.pallas import tpu as pltpu
from jax.sharding import PartitionSpec as P

D = 3072
FF = 12288
TOKENS = 4096
GROUP = 256
ROWS = 192
QUARTER = 384
HALF = 1536

RADIUS_SHARE = 0.5
EPSILON = 1e-06
BF = jnp.bfloat16
F32 = jnp.float32
MESH = pl.DeviceIdType.MESH


def dot(a, b, dims):
    return lax.dot_general(a, b, (dims, ((), ())), preferred_element_type=F32)


def gelu_pair(h):
    cdf = 0.5 * (1.0 + lax.erf(h * (1.0 / math.sqrt(2.0))))
    pdf = jnp.exp(-0.5 * h * h) * (1.0 / math.sqrt(2.0 * math.pi))
    return h * cdf, cdf + h * pdf


def kernel(
    tok_ref, cot_ref, w2_ref, quad_out, input_out,
    X, W, HB, GS, GM, S1, S2, T, HOP, FL, FR, OS, PO, PS, PR, YB, ZA, RA, RB, YA, ZB, IG,
    SQ, SQR, FAC, send, recv, local,
):
    dp, fs = lax.axis_index("dp"), lax.axis_index("fsdp")
    z, ylo = dp // 2, lax.rem(dp, 2)
    yhi, x, c = fs // 8, lax.rem(fs // 2, 4), lax.rem(fs, 2)

    def dev(z, ylo, yhi, x, c):
        return (z * 2 + ylo, yhi * 8 + x * 2 + c)

    right, left, across = lax.rem(x + 1, 4), lax.rem(x + 3, 4), lax.rem(x + 2, 4)
    z_up, z_down, z_far = lax.rem(z + 1, 4), lax.rem(z + 3, 4), lax.rem(z + 2, 4)
    to_sib = dev(z, ylo, yhi, x, 1 - c)
    to_quad = [None, to_sib, dev(z, ylo, 1 - yhi, x, c), dev(z, ylo, 1 - yhi, x, 1 - c)]
    to_right, to_left = dev(z, ylo, yhi, right, c), dev(z, ylo, yhi, left, c)
    to_z = [dev(zz, ylo, yhi, x, c) for zz in (z_up, z_down, z_far)]
    to_yn, to_ym, to_y2 = dev(z, 1 - ylo, 1 - yhi, x, c), dev(z, 1 - ylo, yhi, x, c), to_quad[2]
    to_y = [to_ym, to_yn, to_y2]
    y_of = [(yhi, 1 - ylo), (1 - yhi, 1 - ylo), (1 - yhi, ylo)]
    z_of = [z_up, z_down, z_far]

    count = [0]
    pending = []

    def remote(src, dst, target, keep=True):
        i = count[0]
        count[0] += 1
        copy = pltpu.make_async_remote_copy(
            src_ref=src, dst_ref=dst, send_sem=send.at[i], recv_sem=recv.at[i],
            device_id=target, device_id_type=MESH,
        )
        copy.start()
        if keep:
            pending.append(copy)
        return copy

    member = [(yhi, c), (yhi, 1 - c), (1 - yhi, c), (1 - yhi, 1 - c)]

    def rows_of(xx, j):
        yy, cc = member[j]
        return pl.ds(pl.multiple_of((yy * 8 + xx * 2 + cc) * ROWS, 64), ROWS)

    def quarter_of(j):
        yy, cc = member[j]
        return pl.ds(pl.multiple_of((yy * 2 + cc) * QUARTER, 128), QUARTER)

    def group_rows(j, start=0, size=GROUP):
        yy, cc = member[j]
        return pl.ds(pl.multiple_of((yy * 2 + cc) * GROUP + start, 64), size)

    barrier = pltpu.get_barrier_semaphore()
    peers = [to_sib, to_quad[2], to_quad[3], to_right, to_left, *to_z, to_yn, to_ym]
    copies = [
        pltpu.make_async_copy(tok_ref, X.at[0, group_rows(0)], local.at[0]),
        pltpu.make_async_copy(cot_ref, X.at[1, group_rows(0)], local.at[1]),
        pltpu.make_async_copy(w2_ref.at[:, :, quarter_of(0)], W.at[:, rows_of(x, 0)], local.at[2]),
    ]
    for copy in copies:
        copy.start()
    for peer in peers:
        pl.semaphore_signal(barrier, inc=1, device_id=peer, device_id_type=MESH)
    pl.semaphore_wait(barrier, len(peers))

    quad = [None] + [
        remote(w2_ref.at[:, :, quarter_of(j)], W.at[:, rows_of(x, 0)], to_quad[j]) for j in (2, 3, 1)
    ]
    quad = [None, quad[3], quad[1], quad[2]]
    from_left, from_right = [None] * 4, [None] * 4

    def ring(j):
        block = W.at[:, rows_of(x, j)]
        from_left[j] = remote(block, block, to_right)
        from_right[j] = remote(block, block, to_left)

    def relay_right(j):
        from_left[j].wait_recv()
        block = W.at[:, rows_of(left, j)]
        return remote(block, block, to_right)

    def relay_left(j):
        from_right[j].wait_recv()
        block = W.at[:, rows_of(right, j)]
        return remote(block, block, to_left)

    for copy in copies:
        copy.wait()
    ring(0)
    slice_rows = lambda zz: group_rows(0, zz * 64, 64)
    part_rows = lambda zz: group_rows(2, zz * 64, 64)
    tok_y = [remote(X.at[k, slice_rows(z)], X.at[k, slice_rows(z)], to_yn) for k in (0, 1)]
    tok_c = [remote(X.at[k, group_rows(0)], X.at[k, group_rows(0)], to_sib) for k in (0, 1)]

    def gram(k, rows):
        block = X[k, rows, :]
        g = dot(block, block, ((1,), (1,)))
        hi = g.astype(BF)
        GM[k, 0, rows, :] = hi
        GM[k, 1, rows, :] = (g - hi.astype(F32)).astype(BF)

    def gram_of(j):
        @pl.loop(0, 2)
        def _(k):
            gram(k, group_rows(j))

    quad[1].wait_recv()
    ring(1)
    gram_of(0)
    relays = [relay_right(0), relay_left(1)]
    for copy in tok_c:
        copy.wait_recv()
    gram_of(1)
    tok_up, tok_down, tok_far, tok_fwd = [None] * 2, [None] * 2, [None] * 2, []

    def forward(k, zz):
        block = X.at[k, part_rows(zz)]
        tok_fwd.append(remote(block, block, to_sib))

    def spread(k):
        tok_y[k].wait_recv()
        block = X.at[k, part_rows(z)]
        tok_up[k] = remote(block, block, to_z[0])
        tok_down[k] = remote(block, block, to_z[1])
        forward(k, z)

    spread(0)
    quad[2].wait_recv()
    ring(2)
    quad[3].wait_recv()
    ring(3)
    spread(1)
    tok_up[0].wait_recv()
    block = X.at[0, part_rows(z_down)]
    tok_far[0] = remote(block, block, to_z[0])
    forward(0, z_down)
    tok_down[0].wait_recv()
    forward(0, z_up)
    relays += [relay_right(2)]
    tok_down[1].wait_recv()
    block = X.at[1, part_rows(z_up)]
    tok_far[1] = remote(block, block, to_z[1])
    forward(1, z_up)
    tok_up[1].wait_recv()
    forward(1, z_down)
    relays += [relay_left(3)]
    for k in (0, 1):
        tok_far[k].wait_recv()
        forward(k, z_far)
    for copy in tok_fwd:
        copy.wait_recv()
    gram_of(2)
    gram_of(3)
    for j in (1, 3):
        from_left[j].wait_recv()
    for j in (0, 2):
        from_right[j].wait_recv()
    for copy in relays:
        copy.wait_recv()

    SQ[...] = jnp.zeros_like(SQ)

    @pl.loop(0, 4)
    def _(g):
        rows = pl.ds(pl.multiple_of(g * GROUP, GROUP), GROUP)

        @pl.loop(0, 2)
        def _(k):
            HB[k, rows, :] = dot(X[k, rows, :], W[k], ((1,), (0,)))

        @pl.loop(0, 4)
        def _(s):
            part = pl.ds(pl.multiple_of(g * GROUP + s * 64, 64), 64)
            act, der = gelu_pair(HB[0, part, :])
            S1[0, part, :] = (HB[1, part, :] * der).astype(BF)
            S1[1, part, :] = act.astype(BF)

        @pl.loop(0, 2)
        def _(k):
            s = S1[k, rows, :]
            gs = dot(GM[k, 0, rows, :], s, ((1,), (0,))) + dot(GM[k, 1, rows, :], s, ((1,), (0,)))
            GS[k, rows, :] = gs
            row = jnp.sum(gs * s.astype(F32), axis=0, keepdims=True)
            row = row[:, :128] + row[:, 128:256] + row[:, 256:]
            SQ[pl.ds(g, 1), :] += row

    def exchange(slot, targets):
        got = [remote(SQ, SQR.at[slot + i], t, keep=False) for i, t in enumerate(targets)]
        for copy in got:
            copy.wait_recv()
            copy.wait_send()
        total = SQ[...]
        for i in range(len(targets)):
            total += SQR[slot + i]
        SQ[...] = total

    exchange(0, [to_sib])
    exchange(1, to_y)
    exchange(4, to_z)
    square = jnp.sum(SQ[...], axis=1, keepdims=True)
    FAC[...] = jnp.broadcast_to(RADIUS_SHARE * math.sqrt(D + FF) / jnp.sqrt(square + EPSILON), FAC.shape)

    @pl.loop(0, 16)
    def _(s):
        part = pl.ds(pl.multiple_of(s * 64, 64), 64)
        f = FAC[pl.ds(s // 4, 1), :][:, :1]
        act, der = gelu_pair(HB[0, part, :] + f * GS[0, part, :])
        S2[0, part, :] = ((HB[1, part, :] + f * GS[1, part, :]) * der).astype(BF)
        S2[1, part, :] = act.astype(BF)

    def term(xx, dy):
        yy = yhi if dy == 0 else 1 - yhi
        base = pl.ds(pl.multiple_of((yy * 4 + xx) * QUARTER, 128), QUARTER)

        @pl.loop(0, 2)
        def _(k):
            T[k, base, :] = dot(X[k, :, base], S2[k], ((0,), (0,))).astype(BF)

    def send_term(src_x, j, dst, target):
        return remote(T.at[:, rows_of(src_x, j)], dst, target)

    hop = [None] * 4
    term(across, 1)
    hop[2] = send_term(across, 2, HOP.at[2], to_right)
    hop[3] = send_term(across, 3, HOP.at[3], to_left)
    term(across, 0)
    hop[0] = send_term(across, 0, HOP.at[0], to_right)
    hop[1] = send_term(across, 1, HOP.at[1], to_left)

    def input_rows(yy, cc, dst, add):
        g = yy * 2 + cc
        rows = pl.ds(pl.multiple_of(g * GROUP, GROUP), GROUP)
        f = FAC[pl.ds(g, 1), :][:, :1]
        cross = (f * dot(S2[0, rows, :], S1[0, rows, :], ((1,), (1,)))).astype(BF)

        @pl.loop(0, 4)
        def _(n):
            cols = pl.ds(pl.multiple_of(n * 768, 768), 768)
            out = dot(S2[0, rows, :], W[0, cols, :], ((1,), (1,))) + dot(cross, X[0, rows, cols], ((1,), (0,)))
            out = out.reshape(4, 2, 32, 768)
            if add is not None:
                out = out + add[yy, :, :, :, cols].astype(F32)
            dst[yy, :, :, :, cols] = out.astype(BF)

    to_core = []
    for yy in (0, 1):
        input_rows(yy, 1 - c, PS, None)
        to_core.append(remote(PS.at[yy], PR.at[yy], to_sib))
    final_left, final_right = [None] * 4, [None] * 4
    term(right, 1)
    final_left[3] = send_term(right, 3, FL.at[3], to_right)
    term(left, 1)
    final_right[2] = send_term(left, 2, FR.at[2], to_left)
    for yy in (0, 1):
        to_core[yy].wait_recv()
        input_rows(yy, c, PO, PR)
    lo, hi = pl.ds(0, HALF), pl.ds(HALF, HALF)
    za = [remote(PO.at[:, z_of[i], :, :, lo], ZA.at[i], to_z[i]) for i in range(3)]
    yb = [remote(PO.at[y_of[i][0], :, y_of[i][1], :, hi], YB.at[i], to_y[i]) for i in range(3)]

    def add_hop(xx, j):
        hop[j].wait_recv()
        rows = rows_of(xx, j)
        T[:, rows, :] = (T[:, rows, :].astype(F32) + HOP[j].astype(F32)).astype(BF)

    add_hop(right, 2)
    final_left[2] = send_term(right, 2, FL.at[2], to_right)
    add_hop(left, 3)
    final_right[3] = send_term(left, 3, FR.at[3], to_left)
    term(right, 0)
    final_left[1] = send_term(right, 1, FL.at[1], to_right)
    term(left, 0)
    final_right[0] = send_term(left, 0, FR.at[0], to_left)
    add_hop(right, 0)
    final_left[0] = send_term(right, 0, FL.at[0], to_right)
    add_hop(left, 1)
    final_right[1] = send_term(left, 1, FR.at[1], to_left)
    term(x, 1)
    term(x, 0)

    def total(j):
        final_left[j].wait_recv()
        final_right[j].wait_recv()
        OS[j] = (T[:, rows_of(x, j), :].astype(F32) + FL[j].astype(F32) + FR[j].astype(F32)).astype(BF)

    my_quarter = yhi * 2 + c

    for copy in za:
        copy.wait_recv()

    @pl.loop(0, 4)
    def _(i):
        a, b = i // 2, lax.rem(i, 2)
        s = PO[a, z, b, :, lo].astype(F32)
        for slot in range(3):
            s += ZA[slot, a, b].astype(F32)
        RA[a, b] = s.astype(BF)

    ya = [remote(RA.at[y_of[i][0], y_of[i][1]], YA.at[i], to_y[i]) for i in range(3)]
    for copy in yb:
        copy.wait_recv()

    @pl.loop(0, 4)
    def _(i):
        s = PO[yhi, i, ylo, :, hi].astype(F32)
        for slot in range(3):
            s += YB[slot, i].astype(F32)
        RB[i] = s.astype(BF)

    zb = [remote(RB.at[z_of[i]], ZB.at[i], to_z[i]) for i in range(3)]
    outs = []
    total(2)
    outs.append(remote(OS.at[2], quad_out.at[my_quarter], to_quad[2]))
    total(3)
    outs.append(remote(OS.at[3], quad_out.at[my_quarter], to_quad[3]))
    for copy in ya:
        copy.wait_recv()
    s = RA[yhi, ylo].astype(F32)
    for slot in range(3):
        s += YA[slot].astype(F32)
    IG[z, ylo, :, lo] = s.astype(BF)
    for copy in zb:
        copy.wait_recv()
    s = RB[z].astype(F32)
    for slot in range(3):
        s += ZB[slot].astype(F32)
    IG[z, ylo, :, hi] = s.astype(BF)

    mine = IG.at[z, ylo]
    ig_ym = remote(mine, mine, to_ym)
    ig = [remote(mine, mine, to_z[i]) for i in range(3)]
    total(1)
    outs.append(remote(OS.at[1], quad_out.at[my_quarter], to_quad[1]))
    total(0)
    own = pltpu.make_async_copy(OS.at[0], quad_out.at[my_quarter], local.at[3])
    own.start()
    ig_ym.wait_recv()
    other = IG.at[z, 1 - ylo]
    ig += [remote(other, other, to_z[i]) for i in range(3)]
    for copy in ig:
        copy.wait_recv()
    done = pltpu.make_async_copy(IG, input_out, local.at[4])
    done.start()
    for copy in outs:
        copy.wait_recv()
    own.wait()
    done.wait()
    for copy in pending:
        copy.wait_send()


def on_device(tokens, cotangent, w_in, w_out):
    grad_scale = 1.0 / math.sqrt(TOKENS)
    both = jnp.stack([w_in, w_out.T])
    any_space = pl.BlockSpec(memory_space=pl.ANY)
    vmem = pltpu.VMEM
    sums, input_grad = pl.pallas_call(
        kernel,
        out_shape=(
            jax.ShapeDtypeStruct((4, 2, ROWS, QUARTER), BF),
            jax.ShapeDtypeStruct((4, 2, 32, D), BF),
        ),
        in_specs=[any_space, any_space, pl.BlockSpec(memory_space=pltpu.VMEM)],
        out_specs=(any_space, any_space),
        scratch_shapes=[
            vmem((2, 4 * GROUP, D), BF),
            vmem((2, D, QUARTER), BF),
            vmem((2, 4 * GROUP, QUARTER), F32),
            vmem((2, 4 * GROUP, QUARTER), F32),
            vmem((2, 2, 4 * GROUP, GROUP), BF),
            vmem((2, 4 * GROUP, QUARTER), BF),
            vmem((2, 4 * GROUP, QUARTER), BF),
            vmem((2, D, QUARTER), BF),
            vmem((4, 2, ROWS, QUARTER), BF),
            vmem((4, 2, ROWS, QUARTER), BF),
            vmem((4, 2, ROWS, QUARTER), BF),
            vmem((4, 2, ROWS, QUARTER), BF),
            vmem((2, 4, 2, 32, D), BF),
            vmem((2, 4, 2, 32, D), BF),
            vmem((2, 4, 2, 32, D), BF),
            vmem((3, 4, 32, HALF), BF),
            vmem((3, 2, 2, 32, HALF), BF),
            vmem((2, 2, 32, HALF), BF),
            vmem((4, 32, HALF), BF),
            vmem((3, 32, HALF), BF),
            vmem((3, 32, HALF), BF),
            vmem((4, 2, 32, D), BF),
            vmem((8, 128), F32),
            vmem((7, 8, 128), F32),
            vmem((8, 128), F32),
            pltpu.SemaphoreType.DMA((96,)),
            pltpu.SemaphoreType.DMA((96,)),
            pltpu.SemaphoreType.DMA((5,)),
        ],
        compiler_params=pltpu.CompilerParams(
            collective_id=0, has_side_effects=True, vmem_limit_bytes=63 * 2**20
        ),
        cost_estimate=pl.CostEstimate(flops=20 * 10**9, bytes_accessed=40 * 2**20, transcendentals=10**6),
    )(tokens, cotangent, both)
    grads = sums.transpose(1, 2, 0, 3).reshape(2, ROWS, 4 * QUARTER).astype(F32) * grad_scale
    return grads[0], grads[1].T, input_grad.reshape(GROUP, D)


def solution(mesh):
    return jax.shard_map(
        on_device,
        mesh=mesh,
        in_specs=(P("fsdp", None), P("fsdp", None), P("fsdp", "dp"), P("dp", "fsdp")),
        out_specs=(P("fsdp", "dp"), P("dp", "fsdp"), P("fsdp", None)),
        check_vma=False,
    )
```

```python
import math

import jax
import jax.numpy as jnp
from jax import lax
from jax.experimental import pallas as pl
from jax.experimental.pallas import tpu as pltpu
from jax.sharding import PartitionSpec as P

D = 3072
FF = 12288
TOKENS = 4096
GROUP = 256
ROWS = 192
QUARTER = 384
HALF = 1536

RADIUS_SHARE = 0.5
EPSILON = 1e-06
BF = jnp.bfloat16
F32 = jnp.float32
MESH = pl.DeviceIdType.MESH


def dot(a, b, dims):
    return lax.dot_general(a, b, (dims, ((), ())), preferred_element_type=F32)


def gelu_pair(h):
    cdf = 0.5 * (1.0 + lax.erf(h * (1.0 / math.sqrt(2.0))))
    pdf = jnp.exp(-0.5 * h * h) * (1.0 / math.sqrt(2.0 * math.pi))
    return h * cdf, cdf + h * pdf


def kernel(
    tok_ref, cot_ref, win_ref, wout_ref, gin_out, gout_out, input_out,
    X, W, HB, GS, GM, S1, S2, T, HOP, FL, FR, OS, PO, PS, PR, ZH, ZF, YB, RA, RB, YA, ZB, IG,
    SQ, SQR, FAC, send, recv, local,
):
    dp, fs = lax.axis_index("dp"), lax.axis_index("fsdp")
    z, ylo = dp // 2, lax.rem(dp, 2)
    yhi, x, c = fs // 8, lax.rem(fs // 2, 4), lax.rem(fs, 2)

    def dev(z, ylo, yhi, x, c):
        return (z * 2 + ylo, yhi * 8 + x * 2 + c)

    right, left, across = lax.rem(x + 1, 4), lax.rem(x + 3, 4), lax.rem(x + 2, 4)
    z_up, z_down, z_far = lax.rem(z + 1, 4), lax.rem(z + 3, 4), lax.rem(z + 2, 4)
    to_sib = dev(z, ylo, yhi, x, 1 - c)
    to_quad = [None, to_sib, dev(z, ylo, 1 - yhi, x, c), dev(z, ylo, 1 - yhi, x, 1 - c)]
    to_right, to_left = dev(z, ylo, yhi, right, c), dev(z, ylo, yhi, left, c)
    to_z = [dev(zz, ylo, yhi, x, c) for zz in (z_up, z_down, z_far)]
    to_yn, to_ym, to_y2 = dev(z, 1 - ylo, 1 - yhi, x, c), dev(z, 1 - ylo, yhi, x, c), to_quad[2]
    to_y = [to_ym, to_yn, to_y2]
    y_of = [(yhi, 1 - ylo), (1 - yhi, 1 - ylo), (1 - yhi, ylo)]
    z_of = [z_up, z_down, z_far]

    count = [0]
    pending = []

    def remote(src, dst, target, keep=True):
        i = count[0]
        count[0] += 1
        copy = pltpu.make_async_remote_copy(
            src_ref=src, dst_ref=dst, send_sem=send.at[i], recv_sem=recv.at[i],
            device_id=target, device_id_type=MESH,
        )
        copy.start()
        if keep:
            pending.append(copy)
        return copy

    member = [(yhi, c), (yhi, 1 - c), (1 - yhi, c), (1 - yhi, 1 - c)]

    def rows_of(xx, j):
        yy, cc = member[j]
        return pl.ds(pl.multiple_of((yy * 8 + xx * 2 + cc) * ROWS, 64), ROWS)

    def quarter_of(j):
        yy, cc = member[j]
        return pl.ds(pl.multiple_of((yy * 2 + cc) * QUARTER, 128), QUARTER)

    def group_rows(j, start=0, size=GROUP):
        yy, cc = member[j]
        return pl.ds(pl.multiple_of((yy * 2 + cc) * GROUP + start, 32), size)

    barrier = pltpu.get_barrier_semaphore()
    peers = [to_sib, to_quad[2], to_quad[3], to_right, to_left, *to_z, to_yn, to_ym]
    tokens_of, weights_of = (tok_ref, cot_ref), (win_ref, wout_ref)
    copies = [
        pltpu.make_async_copy(weights_of[k].at[:, quarter_of(0)], W.at[k, rows_of(x, 0)], local.at[k])
        for k in (0, 1)
    ] + [pltpu.make_async_copy(tokens_of[k], X.at[k, group_rows(0)], local.at[2 + k]) for k in (0, 1)]
    for copy in copies:
        copy.start()
    for peer in peers:
        pl.semaphore_signal(barrier, inc=1, device_id=peer, device_id_type=MESH)
    pl.semaphore_wait(barrier, len(peers))

    quad = [None] * 4

    def to_member(j):
        quad[j] = [
            remote(weights_of[k].at[:, quarter_of(j)], W.at[k, rows_of(x, 0)], to_quad[j]) for k in (0, 1)
        ]

    def to_partner(k):
        rows = pl.ds(pl.multiple_of(z * 64 + ylo * 32, 32), 32)
        return remote(tokens_of[k].at[rows], X.at[k, group_rows(0, z * 64 + ylo * 32, 32)], to_yn)

    tok_n = [to_partner(k) for k in (0, 1)]
    to_member(1)
    from_left, from_right = [None] * 4, [None] * 4

    def ring(j):
        block = W.at[:, rows_of(x, j)]
        from_left[j] = remote(block, block, to_right)
        from_right[j] = remote(block, block, to_left)

    def relay_right(j):
        from_left[j].wait_recv()
        block = W.at[:, rows_of(left, j)]
        return remote(block, block, to_right)

    def relay_left(j):
        from_right[j].wait_recv()
        block = W.at[:, rows_of(right, j)]
        return remote(block, block, to_left)

    for copy in copies[:2]:
        copy.wait()
    ring(0)
    for copy in copies[2:]:
        copy.wait()
    tok_c = [remote(X.at[k, group_rows(0)], X.at[k, group_rows(0)], to_sib) for k in (0, 1)]

    def got(copies):
        for copy in copies:
            copy.wait_recv()

    def gram_of(j):
        @pl.loop(0, 2)
        def _(k):
            rows = group_rows(j)
            block = X[k, rows, :]
            g = dot(block, block, ((1,), (1,)))
            hi = g.astype(BF)
            GM[k, 0, rows, :] = hi
            GM[k, 1, rows, :] = (g - hi.astype(F32)).astype(BF)

    def hidden(yy, xx, first=False):
        @pl.loop(0, 4)
        def _(i):
            k = i // 2
            rows = pl.ds(pl.multiple_of((yy * 2 + lax.rem(i, 2)) * GROUP, GROUP), GROUP)
            out = None
            for half in (0, 1):
                base = pl.ds(pl.multiple_of((half * 4 + xx) * QUARTER, 128), QUARTER)
                part = dot(X[k, rows, base], W[k, base, :], ((1,), (0,)))
                out = part if out is None else out + part
            if not first:
                out = out + HB[k, rows, :]
            HB[k, rows, :] = out

    part_rows = lambda zz, yl: group_rows(2, zz * 64 + yl * 32, 32)
    fwd = []
    up, down, far = {}, {}, {}

    def forward(k, zz, yl):
        block = X.at[k, part_rows(zz, yl)]
        fwd.append(remote(block, block, to_sib))

    def spread(k, n):
        yl = 1 - ylo if n == 0 else ylo
        block = X.at[k, part_rows(z, yl)]
        up[k, n] = remote(block, block, to_z[0])
        down[k, n] = remote(block, block, to_z[1])
        forward(k, z, yl)

    def pass_on(k, n):
        yl = 1 - ylo if n == 0 else ylo
        if k == 0:
            up[k, n].wait_recv()
            block = X.at[k, part_rows(z_down, yl)]
            far[k, n] = remote(block, block, to_z[0])
            forward(k, z_down, yl)
        else:
            down[k, n].wait_recv()
            block = X.at[k, part_rows(z_up, yl)]
            far[k, n] = remote(block, block, to_z[1])
            forward(k, z_up, yl)

    def rest(k, n):
        yl = 1 - ylo if n == 0 else ylo
        if k == 0:
            down[k, n].wait_recv()
            forward(k, z_up, yl)
        else:
            up[k, n].wait_recv()
            forward(k, z_down, yl)

    def last(k, n):
        yl = 1 - ylo if n == 0 else ylo
        far[k, n].wait_recv()
        forward(k, z_far, yl)

    tok_m = [None] * 2

    def from_partner(k):
        tok_n[k].wait_recv()
        block = X.at[k, part_rows(z, 1 - ylo)]
        tok_m[k] = remote(block, block, to_ym)
        spread(k, 0)

    got(quad[1])
    ring(1)
    from_partner(0)
    gram_of(0)
    relays = [relay_right(0)]
    from_partner(1)
    to_member(2)
    to_member(3)
    relays += [relay_left(1)]
    tok_m[0].wait_recv()
    spread(0, 1)
    pass_on(0, 0)
    tok_m[1].wait_recv()
    spread(1, 1)
    pass_on(1, 0)
    got(tok_c)
    gram_of(1)
    got(quad[2])
    ring(2)
    rest(0, 0)
    rest(1, 0)
    got(quad[3])
    ring(3)
    hidden(yhi, x, first=True)
    pass_on(0, 1)
    pass_on(1, 1)
    last(0, 0)
    last(1, 0)
    relays += [relay_right(2)]
    rest(0, 1)
    rest(1, 1)
    relays += [relay_left(3)]
    last(0, 1)
    last(1, 1)
    got([from_left[1], from_left[3], from_right[0], from_right[2]])
    hidden(yhi, left)
    hidden(yhi, right)
    got(fwd)
    gram_of(2)
    gram_of(3)
    hidden(1 - yhi, x, first=True)
    hidden(1 - yhi, left)
    hidden(1 - yhi, right)
    got(relays)
    hidden(yhi, across)
    hidden(1 - yhi, across)

    SQ[...] = jnp.zeros_like(SQ)

    @pl.loop(0, 4)
    def _(g):
        rows = pl.ds(pl.multiple_of(g * GROUP, GROUP), GROUP)

        @pl.loop(0, 4)
        def _(s):
            part = pl.ds(pl.multiple_of(g * GROUP + s * 64, 64), 64)
            act, der = gelu_pair(HB[0, part, :])
            S1[0, part, :] = (HB[1, part, :] * der).astype(BF)
            S1[1, part, :] = act.astype(BF)

        @pl.loop(0, 2)
        def _(k):
            s = S1[k, rows, :]
            gs = dot(GM[k, 0, rows, :], s, ((1,), (0,))) + dot(GM[k, 1, rows, :], s, ((1,), (0,)))
            GS[k, rows, :] = gs
            row = jnp.sum(gs * s.astype(F32), axis=0, keepdims=True)
            row = row[:, :128] + row[:, 128:256] + row[:, 256:]
            SQ[pl.ds(g, 1), :] += row

    def exchange(slot, targets):
        sums = [remote(SQ, SQR.at[slot + i], t, keep=False) for i, t in enumerate(targets)]
        for copy in sums:
            copy.wait_recv()
            copy.wait_send()
        total = SQ[...]
        for i in range(len(targets)):
            total += SQR[slot + i]
        SQ[...] = total

    exchange(0, [to_sib])
    exchange(1, to_y)
    exchange(4, to_z)
    square = jnp.sum(SQ[...], axis=1, keepdims=True)
    FAC[...] = jnp.broadcast_to(RADIUS_SHARE * math.sqrt(D + FF) / jnp.sqrt(square + EPSILON), FAC.shape)

    @pl.loop(0, 16)
    def _(s):
        part = pl.ds(pl.multiple_of(s * 64, 64), 64)
        f = FAC[pl.ds(s // 4, 1), :][:, :1]
        act, der = gelu_pair(HB[0, part, :] + f * GS[0, part, :])
        S2[0, part, :] = ((HB[1, part, :] + f * GS[1, part, :]) * der).astype(BF)
        S2[1, part, :] = act.astype(BF)

    def term(xx, dy):
        yy = yhi if dy == 0 else 1 - yhi
        base = pl.ds(pl.multiple_of((yy * 4 + xx) * QUARTER, 128), QUARTER)

        @pl.loop(0, 2)
        def _(k):
            T[k, base, :] = dot(X[k, :, base], S2[k], ((0,), (0,))).astype(BF)

    def send_term(src_x, j, dst, target):
        return remote(T.at[:, rows_of(src_x, j)], dst, target)

    def input_rows(yy, cc, dst, add):
        g = yy * 2 + cc
        rows = pl.ds(pl.multiple_of(g * GROUP, GROUP), GROUP)
        f = FAC[pl.ds(g, 1), :][:, :1]
        cross = (f * dot(S2[0, rows, :], S1[0, rows, :], ((1,), (1,)))).astype(BF)

        @pl.loop(0, 4)
        def _(n):
            cols = pl.ds(pl.multiple_of(n * 768, 768), 768)
            out = dot(S2[0, rows, :], W[0, cols, :], ((1,), (1,))) + dot(cross, X[0, rows, cols], ((1,), (0,)))
            out = out.reshape(4, 2, 32, 768)
            if add is not None:
                out = out + add[yy, :, :, :, cols].astype(F32)
            dst[yy, :, :, :, cols] = out.astype(BF)

    hop = [None] * 4
    to_core = [None] * 2

    def first_rows(yy):
        input_rows(yy, 1 - c, PS, None)
        to_core[yy] = remote(PS.at[yy], PR.at[yy], to_sib)

    final_left, final_right = [None] * 4, [None] * 4
    first_rows(0)
    term(across, 1)
    hop[2] = send_term(across, 2, HOP.at[2], to_right)
    hop[3] = send_term(across, 3, HOP.at[3], to_left)
    first_rows(1)
    term(right, 1)
    final_left[3] = send_term(right, 3, FL.at[3], to_right)
    term(left, 1)
    final_right[2] = send_term(left, 2, FR.at[2], to_left)
    for yy in (0, 1):
        to_core[yy].wait_recv()
        input_rows(yy, c, PO, PR)
    halves, tail = (pl.ds(0, 1024), pl.ds(1024, 1024)), pl.ds(2048, 1024)
    z_hop = [
        remote(PO.at[:, z_far, :, :, halves[0]], ZH.at[0], to_z[0]),
        remote(PO.at[:, z_far, :, :, halves[1]], ZH.at[1], to_z[1]),
    ]
    yb = [remote(PO.at[y_of[i][0], :, y_of[i][1], :, tail], YB.at[i], to_y[i]) for i in range(3)]
    z_own = [
        remote(PO.at[:, z_down, :, :, halves[0]], ZF.at[0, 0], to_z[1]),
        remote(PO.at[:, z_up, :, :, halves[1]], ZF.at[1, 0], to_z[0]),
    ]

    def add_hop(xx, j):
        hop[j].wait_recv()
        rows = rows_of(xx, j)
        T[:, rows, :] = (T[:, rows, :].astype(F32) + HOP[j].astype(F32)).astype(BF)

    add_hop(right, 2)
    final_left[2] = send_term(right, 2, FL.at[2], to_right)
    add_hop(left, 3)
    final_right[3] = send_term(left, 3, FR.at[3], to_left)
    term(across, 0)
    hop[0] = send_term(across, 0, HOP.at[0], to_right)
    hop[1] = send_term(across, 1, HOP.at[1], to_left)
    z_sum = []
    for h, (zz, target) in enumerate(((z_up, to_z[0]), (z_down, to_z[1]))):
        z_hop[h].wait_recv()

        @pl.loop(0, 4)
        def _(i):
            a, b = i // 2, lax.rem(i, 2)
            block = PO[a, zz, b, :, halves[h]].astype(F32) + ZH[h, a, b].astype(F32)
            PO[a, zz, b, :, halves[h]] = block.astype(BF)

        z_sum.append(remote(PO.at[:, zz, :, :, halves[h]], ZF.at[h, 1], target))

    term(right, 0)
    final_left[1] = send_term(right, 1, FL.at[1], to_right)
    term(left, 0)
    final_right[0] = send_term(left, 0, FR.at[0], to_left)
    add_hop(right, 0)
    final_left[0] = send_term(right, 0, FL.at[0], to_right)
    add_hop(left, 1)
    final_right[1] = send_term(left, 1, FR.at[1], to_left)
    term(x, 1)
    term(x, 0)

    def total(j):
        final_left[j].wait_recv()
        final_right[j].wait_recv()
        OS[j] = (T[:, rows_of(x, j), :].astype(F32) + FL[j].astype(F32) + FR[j].astype(F32)).astype(BF)

    outs = []

    def deliver(j):
        total(j)
        mine = quarter_of(0)
        for k, out in enumerate((gin_out, gout_out)):
            if j == 0:
                own = pltpu.make_async_copy(OS.at[0, k], out.at[:, mine], local.at[k])
                own.start()
                kept.append(own)
            else:
                outs.append(remote(OS.at[j, k], out.at[:, mine], to_quad[j]))

    kept = []
    got(yb)

    @pl.loop(0, 4)
    def _(i):
        s = PO[yhi, i, ylo, :, tail].astype(F32)
        for slot in range(3):
            s += YB[slot, i].astype(F32)
        RB[i] = s.astype(BF)

    zb = [remote(RB.at[z_of[i]], ZB.at[i], to_z[i]) for i in range(3)]
    got(z_own)
    got(z_sum)

    @pl.loop(0, 4)
    def _(i):
        a, b = i // 2, lax.rem(i, 2)
        for h in (0, 1):
            s = PO[a, z, b, :, halves[h]].astype(F32)
            s += ZF[h, 0, a, b].astype(F32) + ZF[h, 1, a, b].astype(F32)
            RA[a, b, :, halves[h]] = s.astype(BF)

    ya = [remote(RA.at[y_of[i][0], y_of[i][1]], YA.at[i], to_y[i]) for i in range(3)]
    got(zb)
    s = RB[z].astype(F32)
    for slot in range(3):
        s += ZB[slot].astype(F32)
    IG[z, ylo, :, tail] = s.astype(BF)
    got(ya)
    s = RA[yhi, ylo].astype(F32)
    for slot in range(3):
        s += YA[slot].astype(F32)
    IG[z, ylo, :, pl.ds(0, 2048)] = s.astype(BF)

    ig_up, ig_down, ig_far = [None] * 2, [None] * 2, []

    def ig_spread(n):
        mine = IG.at[z, ylo if n == 0 else 1 - ylo]
        ig_up[n] = remote(mine, mine, to_z[0])
        ig_down[n] = remote(mine, mine, to_z[1])

    def ig_pass_on(n):
        yl = ylo if n == 0 else 1 - ylo
        ig_up[n].wait_recv()
        block = IG.at[z_down, yl, :, pl.ds(0, HALF)]
        ig_far.append(remote(block, block, to_z[0]))
        ig_down[n].wait_recv()
        block = IG.at[z_up, yl, :, pl.ds(HALF, HALF)]
        ig_far.append(remote(block, block, to_z[1]))

    ig_ym = remote(IG.at[z, ylo], IG.at[z, ylo], to_ym)
    ig_spread(0)
    deliver(2)
    deliver(3)
    ig_ym.wait_recv()
    ig_spread(1)
    deliver(1)
    deliver(0)
    ig_pass_on(0)
    ig_pass_on(1)
    got(ig_far)
    done = pltpu.make_async_copy(IG, input_out, local.at[2])
    done.start()
    got(outs)
    for own in kept:
        own.wait()
    done.wait()
    for copy in pending:
        copy.wait_send()


def on_device(tokens, cotangent, w_in, w_out):
    grad_scale = 1.0 / math.sqrt(TOKENS)
    any_space = pl.BlockSpec(memory_space=pl.ANY)
    vmem = pltpu.VMEM
    grad_in, grad_out, input_grad = pl.pallas_call(
        kernel,
        out_shape=(
            jax.ShapeDtypeStruct((ROWS, 4 * QUARTER), BF),
            jax.ShapeDtypeStruct((ROWS, 4 * QUARTER), BF),
            jax.ShapeDtypeStruct((4, 2, 32, D), BF),
        ),
        in_specs=[any_space] * 4,
        out_specs=(any_space,) * 3,
        scratch_shapes=[
            vmem((2, 4 * GROUP, D), BF),
            vmem((2, D, QUARTER), BF),
            vmem((2, 4 * GROUP, QUARTER), F32),
            vmem((2, 4 * GROUP, QUARTER), F32),
            vmem((2, 2, 4 * GROUP, GROUP), BF),
            vmem((2, 4 * GROUP, QUARTER), BF),
            vmem((2, 4 * GROUP, QUARTER), BF),
            vmem((2, D, QUARTER), BF),
            vmem((4, 2, ROWS, QUARTER), BF),
            vmem((4, 2, ROWS, QUARTER), BF),
            vmem((4, 2, ROWS, QUARTER), BF),
            vmem((4, 2, ROWS, QUARTER), BF),
            vmem((2, 4, 2, 32, D), BF),
            vmem((2, 4, 2, 32, D), BF),
            vmem((2, 4, 2, 32, D), BF),
            vmem((2, 2, 2, 32, 1024), BF),
            vmem((2, 2, 2, 2, 32, 1024), BF),
            vmem((3, 4, 32, 1024), BF),
            vmem((2, 2, 32, 2048), BF),
            vmem((4, 32, 1024), BF),
            vmem((3, 32, 2048), BF),
            vmem((3, 32, 1024), BF),
            vmem((4, 2, 32, D), BF),
            vmem((8, 128), F32),
            vmem((7, 8, 128), F32),
            vmem((8, 128), F32),
            pltpu.SemaphoreType.DMA((128,)),
            pltpu.SemaphoreType.DMA((128,)),
            pltpu.SemaphoreType.DMA((4,)),
        ],
        compiler_params=pltpu.CompilerParams(
            collective_id=0, has_side_effects=True, vmem_limit_bytes=63 * 2**20
        ),
        cost_estimate=pl.CostEstimate(flops=20 * 10**9, bytes_accessed=40 * 2**20, transcendentals=10**6),
    )(tokens, cotangent, w_in, w_out.T)
    return (
        grad_in.astype(F32) * grad_scale,
        (grad_out.astype(F32) * grad_scale).T,
        input_grad.reshape(GROUP, D),
    )


def solution(mesh):
    return jax.shard_map(
        on_device,
        mesh=mesh,
        in_specs=(P("fsdp", None), P("fsdp", None), P("fsdp", "dp"), P("dp", "fsdp")),
        out_specs=(P("fsdp", "dp"), P("dp", "fsdp"), P("fsdp", None)),
        check_vma=False,
    )
```

```python
import math

import jax
import jax.numpy as jnp
from jax import lax
from jax.experimental import pallas as pl
from jax.experimental.pallas import tpu as pltpu
from jax.sharding import PartitionSpec as P

D = 3072
FF = 12288
TOKENS = 4096
GROUP = 256
ROWS = 192
QUARTER = 384
CHUNK = 768

RADIUS_SHARE = 0.5
EPSILON = 1e-06
BF = jnp.bfloat16
F32 = jnp.float32
MESH = pl.DeviceIdType.MESH


def dot(a, b, dims):
    return lax.dot_general(a, b, (dims, ((), ())), preferred_element_type=F32)


def gelu_pair(h):
    cdf = 0.5 * (1.0 + lax.erf(h * (1.0 / math.sqrt(2.0))))
    pdf = jnp.exp(-0.5 * h * h) * (1.0 / math.sqrt(2.0 * math.pi))
    return h * cdf, cdf + h * pdf


def kernel(
    tok_ref, cot_ref, win_ref, wout_ref, gin_out, gout_out, input_out,
    X, W, HB, GS, GM, S1, S2, T, HOP, FL, FR, OS, CR, PB, PR, ZH, ZF, RA, YA, IG, ST, SB,
    SQ, SQR, FAC, send, recv, local,
):
    dp, fs = lax.axis_index("dp"), lax.axis_index("fsdp")
    z, ylo = dp // 2, lax.rem(dp, 2)
    yhi, x, c = fs // 8, lax.rem(fs // 2, 4), lax.rem(fs, 2)

    def dev(z, ylo, yhi, x, c):
        return (z * 2 + ylo, yhi * 8 + x * 2 + c)

    right, left, across = lax.rem(x + 1, 4), lax.rem(x + 3, 4), lax.rem(x + 2, 4)
    z_up, z_down, z_far = lax.rem(z + 1, 4), lax.rem(z + 3, 4), lax.rem(z + 2, 4)
    to_sib = dev(z, ylo, yhi, x, 1 - c)
    to_quad = [None, to_sib, dev(z, ylo, 1 - yhi, x, c), dev(z, ylo, 1 - yhi, x, 1 - c)]
    to_right, to_left = dev(z, ylo, yhi, right, c), dev(z, ylo, yhi, left, c)
    to_z = [dev(zz, ylo, yhi, x, c) for zz in (z_up, z_down, z_far)]
    to_yn, to_ym, to_y2 = dev(z, 1 - ylo, 1 - yhi, x, c), dev(z, 1 - ylo, yhi, x, c), to_quad[2]
    to_ynx, to_ymx = dev(z, 1 - ylo, 1 - yhi, x, 1 - c), dev(z, 1 - ylo, yhi, x, 1 - c)
    to_y = [to_ym, to_yn, to_y2]
    y_of = [(yhi, 1 - ylo), (1 - yhi, 1 - ylo), (1 - yhi, ylo)]
    z_of = [z_up, z_down, z_far]

    count = [0]
    pending = []

    def remote(src, dst, target, keep=True):
        i = count[0]
        count[0] += 1
        copy = pltpu.make_async_remote_copy(
            src_ref=src, dst_ref=dst, send_sem=send.at[i], recv_sem=recv.at[i],
            device_id=target, device_id_type=MESH,
        )
        copy.start()
        if keep:
            pending.append(copy)
        return copy

    member = [(yhi, c), (yhi, 1 - c), (1 - yhi, c), (1 - yhi, 1 - c)]

    def rows_of(xx, j):
        yy, cc = member[j]
        return pl.ds(pl.multiple_of((yy * 8 + xx * 2 + cc) * ROWS, 64), ROWS)

    def quarter_of(j):
        yy, cc = member[j]
        return pl.ds(pl.multiple_of((yy * 2 + cc) * QUARTER, 128), QUARTER)

    def group_rows(j, start=0, size=GROUP):
        yy, cc = member[j]
        return pl.ds(pl.multiple_of((yy * 2 + cc) * GROUP + start, 32), size)

    barrier = pltpu.get_barrier_semaphore()
    peers = [to_sib, to_quad[2], to_quad[3], to_right, to_left, *to_z, to_yn, to_ym, to_ynx, to_ymx]
    tokens_of, weights_of = (tok_ref, cot_ref), (win_ref, wout_ref)
    copies = [
        pltpu.make_async_copy(weights_of[k].at[:, quarter_of(0)], W.at[k, rows_of(x, 0)], local.at[k])
        for k in (0, 1)
    ] + [pltpu.make_async_copy(tokens_of[k], X.at[k, group_rows(0)], local.at[2 + k]) for k in (0, 1)]
    for copy in copies:
        copy.start()
    for peer in peers:
        pl.semaphore_signal(barrier, inc=1, device_id=peer, device_id_type=MESH)
    pl.semaphore_wait(barrier, len(peers))

    quad = [None] * 4

    def to_member(j):
        quad[j] = [
            remote(weights_of[k].at[:, quarter_of(j)], W.at[k, rows_of(x, 0)], to_quad[j]) for k in (0, 1)
        ]

    def to_partner(k):
        rows = pl.ds(pl.multiple_of(z * 64 + ylo * 32, 32), 32)
        return remote(tokens_of[k].at[rows], X.at[k, group_rows(0, z * 64 + ylo * 32, 32)], to_yn)

    tok_n = [to_partner(k) for k in (0, 1)]
    stage = {
        j: [remote(weights_of[k].at[:, quarter_of(j)], ST.at[j - 2, k], to_ym) for k in (0, 1)] for j in (2, 3)
    }
    to_member(1)

    def stage_on(j):
        for copy in stage[j]:
            copy.wait_recv()
        quad[j] = [remote(ST.at[j - 2], W.at[:, rows_of(x, 0)], to_yn if j == 2 else to_ynx)]

    from_left, from_right = [None] * 4, [None] * 4

    def ring(j):
        block = W.at[:, rows_of(x, j)]
        from_left[j] = remote(block, block, to_right)
        from_right[j] = remote(block, block, to_left)

    def relay_right(j):
        from_left[j].wait_recv()
        block = W.at[:, rows_of(left, j)]
        return remote(block, block, to_right)

    def relay_left(j):
        from_right[j].wait_recv()
        block = W.at[:, rows_of(right, j)]
        return remote(block, block, to_left)

    for copy in copies[:2]:
        copy.wait()
    ring(0)
    for copy in copies[2:]:
        copy.wait()
    tok_c = [remote(X.at[k, group_rows(0)], X.at[k, group_rows(0)], to_sib) for k in (0, 1)]

    def got(copies):
        for copy in copies:
            copy.wait_recv()

    def gram_of(j):
        @pl.loop(0, 2)
        def _(k):
            rows = group_rows(j)
            block = X[k, rows, :]
            g = dot(block, block, ((1,), (1,)))
            hi = g.astype(BF)
            GM[k, 0, rows, :] = hi
            GM[k, 1, rows, :] = (g - hi.astype(F32)).astype(BF)

    def hidden(yy, xx, half, first=False):
        base = pl.ds(pl.multiple_of((half * 4 + xx) * QUARTER, 128), QUARTER)
        rows = pl.ds(pl.multiple_of(yy * 2 * GROUP, 2 * GROUP), 2 * GROUP)

        @pl.loop(0, 2)
        def _(k):
            out = dot(X[k, rows, base], W[k, base, :], ((1,), (0,)))
            if not first:
                out = out + HB[k, rows, :]
            HB[k, rows, :] = out

    part_rows = lambda zz, yl: group_rows(2, zz * 64 + yl * 32, 32)
    fwd = []
    up, down, far = {}, {}, {}

    def forward(k, zz, yl):
        block = X.at[k, part_rows(zz, yl)]
        fwd.append(remote(block, block, to_sib))

    def spread(k, n):
        yl = 1 - ylo if n == 0 else ylo
        block = X.at[k, part_rows(z, yl)]
        up[k, n] = remote(block, block, to_z[0])
        down[k, n] = remote(block, block, to_z[1])
        forward(k, z, yl)

    def pass_on(k, n):
        yl = 1 - ylo if n == 0 else ylo
        if k == 0:
            up[k, n].wait_recv()
            block = X.at[k, part_rows(z_down, yl)]
            far[k, n] = remote(block, block, to_z[0])
            forward(k, z_down, yl)
        else:
            down[k, n].wait_recv()
            block = X.at[k, part_rows(z_up, yl)]
            far[k, n] = remote(block, block, to_z[1])
            forward(k, z_up, yl)

    def rest(k, n):
        yl = 1 - ylo if n == 0 else ylo
        if k == 0:
            down[k, n].wait_recv()
            forward(k, z_up, yl)
        else:
            up[k, n].wait_recv()
            forward(k, z_down, yl)

    def last(k, n):
        yl = 1 - ylo if n == 0 else ylo
        far[k, n].wait_recv()
        forward(k, z_far, yl)

    tok_m = [None] * 2

    def from_partner(k):
        tok_n[k].wait_recv()
        block = X.at[k, part_rows(z, 1 - ylo)]
        tok_m[k] = remote(block, block, to_ym)
        spread(k, 0)

    other = 1 - yhi
    got(quad[1])
    ring(1)
    from_partner(0)
    gram_of(0)
    relays = [relay_right(0)]
    stage_on(2)
    from_partner(1)
    pass_on(0, 0)
    relays += [relay_left(1)]
    stage_on(3)
    rest(0, 0)
    pass_on(1, 0)
    got(tok_c)
    gram_of(1)
    got(quad[2])
    ring(2)
    tok_m[0].wait_recv()
    spread(0, 1)
    rest(1, 0)
    hidden(yhi, x, yhi, first=True)
    tok_m[1].wait_recv()
    spread(1, 1)
    last(0, 0)
    last(1, 0)
    got(quad[3])
    ring(3)
    got([from_left[1], from_right[0]])
    hidden(yhi, left, yhi)
    pass_on(0, 1)
    hidden(yhi, right, yhi)
    got(relays)
    hidden(yhi, across, yhi)
    pass_on(1, 1)
    rest(0, 1)
    rest(1, 1)
    hidden(yhi, x, other)
    late = [relay_right(2), relay_left(3)]
    last(0, 1)
    last(1, 1)
    got([from_left[3], from_right[2]])
    hidden(yhi, left, other)
    hidden(yhi, right, other)
    got(fwd)
    gram_of(2)
    gram_of(3)
    hidden(other, x, yhi, first=True)
    hidden(other, left, yhi)
    hidden(other, right, yhi)
    hidden(other, across, yhi)
    hidden(other, x, other)
    hidden(other, left, other)
    hidden(other, right, other)
    got(late)
    hidden(yhi, across, other)
    hidden(other, across, other)

    SQ[...] = jnp.zeros_like(SQ)

    @pl.loop(0, 4)
    def _(g):
        rows = pl.ds(pl.multiple_of(g * GROUP, GROUP), GROUP)

        @pl.loop(0, 4)
        def _(s):
            part = pl.ds(pl.multiple_of(g * GROUP + s * 64, 64), 64)
            act, der = gelu_pair(HB[0, part, :])
            S1[0, part, :] = (HB[1, part, :] * der).astype(BF)
            S1[1, part, :] = act.astype(BF)

        @pl.loop(0, 2)
        def _(k):
            s = S1[k, rows, :]
            gs = dot(GM[k, 0, rows, :], s, ((1,), (0,))) + dot(GM[k, 1, rows, :], s, ((1,), (0,)))
            GS[k, rows, :] = gs
            row = jnp.sum(gs * s.astype(F32), axis=0, keepdims=True)
            row = row[:, :128] + row[:, 128:256] + row[:, 256:]
            SQ[pl.ds(g, 1), :] += row

    def exchange(slot, targets):
        sums = [remote(SQ, SQR.at[slot + i], t, keep=False) for i, t in enumerate(targets)]
        for copy in sums:
            copy.wait_recv()
            copy.wait_send()
        total = SQ[...]
        for i in range(len(targets)):
            total += SQR[slot + i]
        SQ[...] = total

    exchange(0, [to_sib])
    exchange(1, to_y)
    exchange(4, to_z)
    square = jnp.sum(SQ[...], axis=1, keepdims=True)
    FAC[...] = jnp.broadcast_to(RADIUS_SHARE * math.sqrt(D + FF) / jnp.sqrt(square + EPSILON), FAC.shape)

    @pl.loop(0, 16)
    def _(s):
        part = pl.ds(pl.multiple_of(s * 64, 64), 64)
        f = FAC[pl.ds(s // 4, 1), :][:, :1]
        act, der = gelu_pair(HB[0, part, :] + f * GS[0, part, :])
        S2[0, part, :] = ((HB[1, part, :] + f * GS[1, part, :]) * der).astype(BF)
        S2[1, part, :] = act.astype(BF)

    def term(xx, dy):
        yy = yhi if dy == 0 else 1 - yhi
        base = pl.ds(pl.multiple_of((yy * 4 + xx) * QUARTER, 128), QUARTER)

        @pl.loop(0, 2)
        def _(k):
            T[k, base, :] = dot(X[k, :, base], S2[k], ((0,), (0,))).astype(BF)

    def send_term(src_x, j, dst, target):
        return remote(T.at[:, rows_of(src_x, j)], dst, target)

    hop, final_left, final_right = [None] * 4, [None] * 4, [None] * 4

    def add_hop(xx, j):
        hop[j].wait_recv()
        rows = rows_of(xx, j)
        T[:, rows, :] = (T[:, rows, :].astype(F32) + HOP[j].astype(F32)).astype(BF)

    def first_hops(j):
        term(across, j // 2)
        hop[j] = send_term(across, j, HOP.at[j], to_right)
        hop[j + 1] = send_term(across, j + 1, HOP.at[j + 1], to_left)

    def directs(j):
        term(right, j // 2)
        final_left[j + 1] = send_term(right, j + 1, FL.at[j + 1], to_right)
        term(left, j // 2)
        final_right[j] = send_term(left, j, FR.at[j], to_left)

    def sums(j):
        add_hop(right, j)
        final_left[j] = send_term(right, j, FL.at[j], to_right)
        add_hop(left, j + 1)
        final_right[j + 1] = send_term(left, j + 1, FR.at[j + 1], to_left)

    def total(j):
        final_left[j].wait_recv()
        final_right[j].wait_recv()
        OS[j] = (T[:, rows_of(x, j), :].astype(F32) + FL[j].astype(F32) + FR[j].astype(F32)).astype(BF)

    outs, kept, staged = [], [], {}
    grad_outs = (gin_out, gout_out)

    def deliver(j):
        total(j)
        if j >= 2:
            staged[j] = remote(OS.at[j], SB.at[j - 2], to_yn)
            return
        for k in (0, 1):
            place = grad_outs[k].at[:, quarter_of(0)]
            if j == 0:
                own = pltpu.make_async_copy(OS.at[0, k], place, local.at[k])
                own.start()
                kept.append(own)
            else:
                outs.append(remote(OS.at[1, k], place, to_sib))

    def deliver_on(j):
        staged[j].wait_recv()
        for k in (0, 1):
            place = grad_outs[k].at[:, quarter_of(2)]
            outs.append(remote(SB.at[j - 2, k], place, to_ym if j == 2 else to_ymx))

    @pl.loop(0, 4)
    def _(g):
        rows = pl.ds(pl.multiple_of(g * GROUP, GROUP), GROUP)
        f = FAC[pl.ds(g, 1), :][:, :1]
        CR[rows, :] = (f * dot(S2[0, rows, :], S1[0, rows, :], ((1,), (1,)))).astype(BF)

    to_core, z_hop, z_own, z_sum, y_part = {}, {}, {}, {}, {}

    def cols_of(n):
        return pl.ds(n * CHUNK, CHUNK)

    def half_of(n, h):
        return pl.ds(n * CHUNK + h * (CHUNK // 2), CHUNK // 2)

    def partial(n):
        cols = cols_of(n)

        @pl.loop(0, 2)
        def _(yy):
            rows = pl.ds(pl.multiple_of(yy * 2 * GROUP, 2 * GROUP), 2 * GROUP)
            out = dot(S2[0, rows, :], W[0, cols, :], ((1,), (1,)))
            for cc in (0, 1):
                group = pl.ds(pl.multiple_of((yy * 2 + cc) * GROUP, GROUP), GROUP)
                mine = out[cc * GROUP : (cc + 1) * GROUP]
                mine = mine + dot(CR[group, :], X[0, group, cols], ((1,), (0,)))
                PB[yy, cc, :, :, :, cols] = mine.reshape(4, 2, 32, CHUNK).astype(BF)

        to_core[n] = remote(PB.at[:, 1 - c, :, :, :, cols], PR.at[:, :, :, :, cols], to_sib)

    def over_z(n):
        cols = cols_of(n)
        to_core[n].wait_recv()

        @pl.loop(0, 8)
        def _(i):
            a, b = i // 4, lax.rem(i, 4)
            both = PB[a, c, b, :, :, cols].astype(F32) + PR[a, b, :, :, cols].astype(F32)
            PB[a, c, b, :, :, cols] = both.astype(BF)

        part = lambda zz, h: PB.at[:, c, zz, :, :, half_of(n, h)]
        z_hop[n] = [remote(part(z_far, h), ZH.at[n, h], to_z[h]) for h in (0, 1)]
        z_own[n] = [remote(part(z_down, 0), ZF.at[n, 0, 0], to_z[1]), remote(part(z_up, 1), ZF.at[n, 1, 0], to_z[0])]

    def z_relay(n):
        z_sum[n] = []
        for h, zz in enumerate((z_up, z_down)):
            z_hop[n][h].wait_recv()
            cols = half_of(n, h)
            both = PB[:, c, zz, :, :, cols].astype(F32) + ZH[n, h].astype(F32)
            PB[:, c, zz, :, :, cols] = both.astype(BF)
            z_sum[n].append(remote(PB.at[:, c, zz, :, :, cols], ZF.at[n, h, 1], to_z[h]))

    def over_y(n):
        got(z_own[n])
        got(z_sum[n])
        for h in (0, 1):
            cols = half_of(n, h)
            s = PB[:, c, z, :, :, cols].astype(F32) + ZF[n, h, 0].astype(F32) + ZF[n, h, 1].astype(F32)
            RA[:, :, :, cols] = s.astype(BF)
        y_part[n] = [remote(RA.at[y_of[i][0], y_of[i][1], :, cols_of(n)], YA.at[n, i], to_y[i]) for i in range(3)]

    ig_ym, ig_up, ig_down, ig_far = {}, {}, {}, []

    def ig_send(n, m):
        mine = IG.at[z, ylo if m == 0 else 1 - ylo, :, cols_of(n)]
        ig_up[n, m] = remote(mine, mine, to_z[0])
        ig_down[n, m] = remote(mine, mine, to_z[1])

    def spread_rows(n):
        got(y_part[n])
        s = RA[yhi, ylo, :, cols_of(n)].astype(F32)
        for slot in range(3):
            s += YA[n, slot].astype(F32)
        IG[z, ylo, :, cols_of(n)] = s.astype(BF)
        mine = IG.at[z, ylo, :, cols_of(n)]
        ig_ym[n] = remote(mine, mine, to_ym)
        ig_send(n, 0)

    def spread_other(n):
        ig_ym[n].wait_recv()
        ig_send(n, 1)

    def spread_far(n, m):
        yl = ylo if m == 0 else 1 - ylo
        ig_up[n, m].wait_recv()
        block = IG.at[z_down, yl, :, half_of(n, 0)]
        ig_far.append(remote(block, block, to_z[0]))
        ig_down[n, m].wait_recv()
        block = IG.at[z_up, yl, :, half_of(n, 1)]
        ig_far.append(remote(block, block, to_z[1]))

    partial(0)
    first_hops(2)
    over_z(0)
    partial(1)
    directs(2)
    over_z(1)
    z_relay(0)
    partial(2)
    sums(2)
    over_z(2)
    first_hops(0)
    z_relay(1)
    over_y(0)
    partial(3)
    directs(0)
    over_z(3)
    z_relay(2)
    over_y(1)
    spread_rows(0)
    term(x, 1)
    deliver(2)
    z_relay(3)
    over_y(2)
    spread_other(0)
    spread_rows(1)
    deliver(3)
    sums(0)
    spread_far(0, 0)
    spread_far(0, 1)
    over_y(3)
    spread_other(1)
    spread_rows(2)
    deliver_on(2)
    term(x, 0)
    spread_far(1, 0)
    spread_far(1, 1)
    spread_other(2)
    spread_rows(3)
    deliver_on(3)
    spread_far(2, 0)
    spread_far(2, 1)
    spread_other(3)
    deliver(1)
    deliver(0)
    spread_far(3, 0)
    spread_far(3, 1)
    got(ig_far)
    done = pltpu.make_async_copy(IG, input_out, local.at[2])
    done.start()
    got(outs)
    for own in kept:
        own.wait()
    done.wait()
    for copy in pending:
        copy.wait_send()


def on_device(tokens, cotangent, w_in, w_out):
    grad_scale = 1.0 / math.sqrt(TOKENS)
    any_space = pl.BlockSpec(memory_space=pl.ANY)
    vmem = pltpu.VMEM
    grad_in, grad_out, input_grad = pl.pallas_call(
        kernel,
        out_shape=(
            jax.ShapeDtypeStruct((ROWS, 4 * QUARTER), BF),
            jax.ShapeDtypeStruct((ROWS, 4 * QUARTER), BF),
            jax.ShapeDtypeStruct((4, 2, 32, D), BF),
        ),
        in_specs=[any_space] * 4,
        out_specs=(any_space,) * 3,
        scratch_shapes=[
            vmem((2, 4 * GROUP, D), BF),
            vmem((2, D, QUARTER), BF),
            vmem((2, 4 * GROUP, QUARTER), F32),
            vmem((2, 4 * GROUP, QUARTER), F32),
            vmem((2, 2, 4 * GROUP, GROUP), BF),
            vmem((2, 4 * GROUP, QUARTER), BF),
            vmem((2, 4 * GROUP, QUARTER), BF),
            vmem((2, D, QUARTER), BF),
            vmem((4, 2, ROWS, QUARTER), BF),
            vmem((4, 2, ROWS, QUARTER), BF),
            vmem((4, 2, ROWS, QUARTER), BF),
            vmem((4, 2, ROWS, QUARTER), BF),
            vmem((4 * GROUP, GROUP), BF),
            vmem((2, 2, 4, 2, 32, D), BF),
            vmem((2, 4, 2, 32, D), BF),
            vmem((4, 2, 2, 2, 32, CHUNK // 2), BF),
            vmem((4, 2, 2, 2, 2, 32, CHUNK // 2), BF),
            vmem((2, 2, 32, D), BF),
            vmem((4, 3, 32, CHUNK), BF),
            vmem((4, 2, 32, D), BF),
            vmem((2, 2, ROWS, QUARTER), BF),
            vmem((2, 2, ROWS, QUARTER), BF),
            vmem((8, 128), F32),
            vmem((7, 8, 128), F32),
            vmem((8, 128), F32),
            pltpu.SemaphoreType.DMA((192,)),
            pltpu.SemaphoreType.DMA((192,)),
            pltpu.SemaphoreType.DMA((4,)),
        ],
        compiler_params=pltpu.CompilerParams(
            collective_id=0, has_side_effects=True, vmem_limit_bytes=63 * 2**20
        ),
        cost_estimate=pl.CostEstimate(flops=20 * 10**9, bytes_accessed=40 * 2**20, transcendentals=10**6),
    )(tokens, cotangent, w_in, w_out.T)
    return (
        grad_in.astype(F32) * grad_scale,
        (grad_out.astype(F32) * grad_scale).T,
        input_grad.reshape(GROUP, D),
    )


def solution(mesh):
    return jax.shard_map(
        on_device,
        mesh=mesh,
        in_specs=(P("fsdp", None), P("fsdp", None), P("fsdp", "dp"), P("dp", "fsdp")),
        out_specs=(P("fsdp", "dp"), P("dp", "fsdp"), P("fsdp", None)),
        check_vma=False,
    )
```

```python
import math

import jax
import jax.numpy as jnp
from jax import lax
from jax.experimental import pallas as pl
from jax.experimental.pallas import tpu as pltpu
from jax.sharding import PartitionSpec as P

D = 3072
FF = 12288
TOKENS = 4096
GROUP = 256
ROWS = 192
QUARTER = 384
CHUNK = 768

RADIUS_SHARE = 0.5
EPSILON = 1e-06
BF = jnp.bfloat16
F32 = jnp.float32
MESH = pl.DeviceIdType.MESH


def dot(a, b, dims):
    return lax.dot_general(a, b, (dims, ((), ())), preferred_element_type=F32)


def gelu_pair(h):
    cdf = 0.5 * (1.0 + lax.erf(h * (1.0 / math.sqrt(2.0))))
    pdf = jnp.exp(-0.5 * h * h) * (1.0 / math.sqrt(2.0 * math.pi))
    return h * cdf, cdf + h * pdf


def kernel(
    tok_ref, cot_ref, win_ref, wout_ref, gin_out, gout_out, input_out,
    X, W, HB, GS, GM, S1, S2, T, HOP, FL, FR, OS, CR, PB, PR, ZH, ZF, RA, YA, IG, ST, SB,
    SQ, SQR, FAC, send, recv, local,
):
    dp, fs = lax.axis_index("dp"), lax.axis_index("fsdp")
    z, ylo = dp // 2, lax.rem(dp, 2)
    yhi, x, c = fs // 8, lax.rem(fs // 2, 4), lax.rem(fs, 2)

    def dev(z, ylo, yhi, x, c):
        return (z * 2 + ylo, yhi * 8 + x * 2 + c)

    right, left, across = lax.rem(x + 1, 4), lax.rem(x + 3, 4), lax.rem(x + 2, 4)
    z_up, z_down, z_far = lax.rem(z + 1, 4), lax.rem(z + 3, 4), lax.rem(z + 2, 4)
    to_sib = dev(z, ylo, yhi, x, 1 - c)
    to_quad = [None, to_sib, dev(z, ylo, 1 - yhi, x, c), dev(z, ylo, 1 - yhi, x, 1 - c)]
    to_right, to_left = dev(z, ylo, yhi, right, c), dev(z, ylo, yhi, left, c)
    to_z = [dev(zz, ylo, yhi, x, c) for zz in (z_up, z_down, z_far)]
    to_yn, to_ym, to_y2 = dev(z, 1 - ylo, 1 - yhi, x, c), dev(z, 1 - ylo, yhi, x, c), to_quad[2]
    to_ynx, to_ymx = dev(z, 1 - ylo, 1 - yhi, x, 1 - c), dev(z, 1 - ylo, yhi, x, 1 - c)
    to_y = [to_ym, to_yn, to_y2]
    y_of = [(yhi, 1 - ylo), (1 - yhi, 1 - ylo), (1 - yhi, ylo)]
    z_of = [z_up, z_down, z_far]

    count = [0]
    pending = []

    def remote(src, dst, target, keep=True):
        i = count[0]
        count[0] += 1
        copy = pltpu.make_async_remote_copy(
            src_ref=src, dst_ref=dst, send_sem=send.at[i], recv_sem=recv.at[i],
            device_id=target, device_id_type=MESH,
        )
        copy.start()
        if keep:
            pending.append(copy)
        return copy

    member = [(yhi, c), (yhi, 1 - c), (1 - yhi, c), (1 - yhi, 1 - c)]

    def rows_of(xx, j):
        yy, cc = member[j]
        return pl.ds(pl.multiple_of((yy * 8 + xx * 2 + cc) * ROWS, 64), ROWS)

    def quarter_of(j):
        yy, cc = member[j]
        return pl.ds(pl.multiple_of((yy * 2 + cc) * QUARTER, 128), QUARTER)

    def group_rows(j, start=0, size=GROUP):
        yy, cc = member[j]
        return pl.ds(pl.multiple_of((yy * 2 + cc) * GROUP + start, 32), size)

    barrier = pltpu.get_barrier_semaphore()
    peers = [to_sib, to_quad[2], to_quad[3], to_right, to_left, *to_z, to_yn, to_ym, to_ynx, to_ymx]
    tokens_of, weights_of = (tok_ref, cot_ref), (win_ref, wout_ref)
    copies = [
        pltpu.make_async_copy(weights_of[k].at[:, quarter_of(0)], W.at[k, rows_of(x, 0)], local.at[k])
        for k in (0, 1)
    ] + [pltpu.make_async_copy(tokens_of[k], X.at[k, group_rows(0)], local.at[2 + k]) for k in (0, 1)]
    for copy in copies:
        copy.start()
    for peer in peers:
        pl.semaphore_signal(barrier, inc=1, device_id=peer, device_id_type=MESH)
    pl.semaphore_wait(barrier, len(peers))

    quad = [None] * 4

    def to_member(j):
        quad[j] = [
            remote(weights_of[k].at[:, quarter_of(j)], W.at[k, rows_of(x, 0)], to_quad[j]) for k in (0, 1)
        ]

    def to_partner(k):
        rows = pl.ds(pl.multiple_of(z * 64 + ylo * 32, 32), 32)
        return remote(tokens_of[k].at[rows], X.at[k, group_rows(0, z * 64 + ylo * 32, 32)], to_yn)

    tok_n = [to_partner(k) for k in (0, 1)]
    stage = {
        j: [remote(weights_of[k].at[:, quarter_of(j)], ST.at[j - 2, k], to_ym) for k in (0, 1)] for j in (2, 3)
    }
    to_member(1)

    def stage_on(j):
        for copy in stage[j]:
            copy.wait_recv()
        quad[j] = [remote(ST.at[j - 2], W.at[:, rows_of(x, 0)], to_yn if j == 2 else to_ynx)]

    from_left, from_right = [None] * 4, [None] * 4

    def ring(j):
        block = W.at[:, rows_of(x, j)]
        from_left[j] = remote(block, block, to_right)
        from_right[j] = remote(block, block, to_left)

    def relay_right(j):
        from_left[j].wait_recv()
        block = W.at[:, rows_of(left, j)]
        return remote(block, block, to_right)

    def relay_left(j):
        from_right[j].wait_recv()
        block = W.at[:, rows_of(right, j)]
        return remote(block, block, to_left)

    for copy in copies[:2]:
        copy.wait()
    ring(0)
    for copy in copies[2:]:
        copy.wait()
    tok_c = [remote(X.at[k, group_rows(0)], X.at[k, group_rows(0)], to_sib) for k in (0, 1)]

    def got(copies):
        for copy in copies:
            copy.wait_recv()

    def gram_of(j):
        @pl.loop(0, 2)
        def _(k):
            rows = group_rows(j)
            block = X[k, rows, :]
            g = dot(block, block, ((1,), (1,)))
            hi = g.astype(BF)
            GM[k, 0, rows, :] = hi
            GM[k, 1, rows, :] = (g - hi.astype(F32)).astype(BF)

    def hidden(yy, xx, half, first=False, both=False):
        base = pl.ds(pl.multiple_of((half * 4 + xx) * QUARTER, 128), QUARTER)
        rows = pl.ds(pl.multiple_of(yy * 2 * GROUP, 2 * GROUP), 2 * GROUP)

        @pl.loop(0, 2)
        def _(k):
            out = dot(X[k, rows, base], W[k, base, :], ((1,), (0,)))
            if both:
                rest = pl.ds(pl.multiple_of((4 + xx) * QUARTER, 128), QUARTER)
                out = out + dot(X[k, rows, rest], W[k, rest, :], ((1,), (0,)))
            if not first:
                out = out + HB[k, rows, :]
            HB[k, rows, :] = out

    part_rows = lambda zz, yl: group_rows(2, zz * 64 + yl * 32, 32)
    fwd = []
    up, down, far = {}, {}, {}

    def forward(k, zz, yl):
        block = X.at[k, part_rows(zz, yl)]
        fwd.append(remote(block, block, to_sib))

    def spread(k, n):
        yl = 1 - ylo if n == 0 else ylo
        block = X.at[k, part_rows(z, yl)]
        up[k, n] = remote(block, block, to_z[0])
        down[k, n] = remote(block, block, to_z[1])
        forward(k, z, yl)

    def pass_on(k, n):
        yl = 1 - ylo if n == 0 else ylo
        if k == 0:
            up[k, n].wait_recv()
            block = X.at[k, part_rows(z_down, yl)]
            far[k, n] = remote(block, block, to_z[0])
            forward(k, z_down, yl)
        else:
            down[k, n].wait_recv()
            block = X.at[k, part_rows(z_up, yl)]
            far[k, n] = remote(block, block, to_z[1])
            forward(k, z_up, yl)

    def rest(k, n):
        yl = 1 - ylo if n == 0 else ylo
        if k == 0:
            down[k, n].wait_recv()
            forward(k, z_up, yl)
        else:
            up[k, n].wait_recv()
            forward(k, z_down, yl)

    def last(k, n):
        yl = 1 - ylo if n == 0 else ylo
        far[k, n].wait_recv()
        forward(k, z_far, yl)

    tok_m = [None] * 2

    def from_partner(k):
        tok_n[k].wait_recv()
        block = X.at[k, part_rows(z, 1 - ylo)]
        tok_m[k] = remote(block, block, to_ym)
        spread(k, 0)

    other = 1 - yhi
    got(quad[1])
    ring(1)
    from_partner(0)
    gram_of(0)
    relays = [relay_right(0)]
    stage_on(2)
    from_partner(1)
    pass_on(0, 0)
    relays += [relay_left(1)]
    stage_on(3)
    rest(0, 0)
    pass_on(1, 0)
    got(tok_c)
    gram_of(1)
    got(quad[2])
    ring(2)
    tok_m[0].wait_recv()
    spread(0, 1)
    rest(1, 0)
    hidden(yhi, x, yhi, first=True)
    tok_m[1].wait_recv()
    spread(1, 1)
    last(0, 0)
    last(1, 0)
    got(quad[3])
    ring(3)
    got([from_left[1], from_right[0]])
    hidden(yhi, left, yhi)
    pass_on(0, 1)
    hidden(yhi, right, yhi)
    got(relays)
    hidden(yhi, across, yhi)
    pass_on(1, 1)
    rest(0, 1)
    rest(1, 1)
    hidden(yhi, x, other)
    late = [relay_right(2), relay_left(3)]
    last(0, 1)
    last(1, 1)
    got([from_left[3], from_right[2]])
    hidden(yhi, left, other)
    hidden(yhi, right, other)
    got(fwd)
    gram_of(2)
    gram_of(3)
    hidden(other, x, 0, first=True, both=True)
    hidden(other, left, 0, both=True)
    hidden(other, right, 0, both=True)
    hidden(other, across, yhi)
    got(late)
    hidden(yhi, across, other)
    hidden(other, across, other)

    SQ[...] = jnp.zeros_like(SQ)

    @pl.loop(0, 4)
    def _(g):
        rows = pl.ds(pl.multiple_of(g * GROUP, GROUP), GROUP)

        @pl.loop(0, 4)
        def _(s):
            part = pl.ds(pl.multiple_of(g * GROUP + s * 64, 64), 64)
            act, der = gelu_pair(HB[0, part, :])
            S1[0, part, :] = (HB[1, part, :] * der).astype(BF)
            S1[1, part, :] = act.astype(BF)

        @pl.loop(0, 2)
        def _(k):
            s = S1[k, rows, :]
            gs = dot(GM[k, 0, rows, :], s, ((1,), (0,))) + dot(GM[k, 1, rows, :], s, ((1,), (0,)))
            GS[k, rows, :] = gs
            row = jnp.sum(gs * s.astype(F32), axis=0, keepdims=True)
            row = row[:, :128] + row[:, 128:256] + row[:, 256:]
            SQ[pl.ds(g, 1), :] += row

    def exchange(slot, targets):
        sums = [remote(SQ, SQR.at[slot + i], t, keep=False) for i, t in enumerate(targets)]
        for copy in sums:
            copy.wait_recv()
            copy.wait_send()
        total = SQ[...]
        for i in range(len(targets)):
            total += SQR[slot + i]
        SQ[...] = total

    exchange(0, [to_sib, *to_y, to_quad[3], to_ynx, to_ymx])
    exchange(7, to_z)
    square = jnp.sum(SQ[...], axis=1, keepdims=True)
    FAC[...] = jnp.broadcast_to(RADIUS_SHARE * math.sqrt(D + FF) / jnp.sqrt(square + EPSILON), FAC.shape)

    @pl.loop(0, 16)
    def _(s):
        part = pl.ds(pl.multiple_of(s * 64, 64), 64)
        f = FAC[pl.ds(s // 4, 1), :][:, :1]
        act, der = gelu_pair(HB[0, part, :] + f * GS[0, part, :])
        S2[0, part, :] = ((HB[1, part, :] + f * GS[1, part, :]) * der).astype(BF)
        S2[1, part, :] = act.astype(BF)

    def term(xx, dy):
        yy = yhi if dy == 0 else 1 - yhi
        base = pl.ds(pl.multiple_of((yy * 4 + xx) * QUARTER, 128), QUARTER)

        @pl.loop(0, 2)
        def _(k):
            T[k, base, :] = dot(X[k, :, base], S2[k], ((0,), (0,))).astype(BF)

    def send_term(src_x, j, dst, target):
        return remote(T.at[:, rows_of(src_x, j)], dst, target)

    hop, final_left, final_right = [None] * 4, [None] * 4, [None] * 4

    def add_hop(xx, j):
        hop[j].wait_recv()
        rows = rows_of(xx, j)
        T[:, rows, :] = (T[:, rows, :].astype(F32) + HOP[j].astype(F32)).astype(BF)

    def first_hops(j):
        term(across, j // 2)
        hop[j] = send_term(across, j, HOP.at[j], to_right)
        hop[j + 1] = send_term(across, j + 1, HOP.at[j + 1], to_left)

    def directs(j):
        term(right, j // 2)
        final_left[j + 1] = send_term(right, j + 1, FL.at[j + 1], to_right)
        term(left, j // 2)
        final_right[j] = send_term(left, j, FR.at[j], to_left)

    def sums(j):
        add_hop(right, j)
        final_left[j] = send_term(right, j, FL.at[j], to_right)
        add_hop(left, j + 1)
        final_right[j + 1] = send_term(left, j + 1, FR.at[j + 1], to_left)

    def total(j):
        final_left[j].wait_recv()
        final_right[j].wait_recv()
        OS[j] = (T[:, rows_of(x, j), :].astype(F32) + FL[j].astype(F32) + FR[j].astype(F32)).astype(BF)

    outs, kept, staged = [], [], {}
    grad_outs = (gin_out, gout_out)

    def deliver(j):
        total(j)
        if j >= 2:
            staged[j] = remote(OS.at[j], SB.at[j - 2], to_yn)
            return
        for k in (0, 1):
            place = grad_outs[k].at[:, quarter_of(0)]
            if j == 0:
                own = pltpu.make_async_copy(OS.at[0, k], place, local.at[k])
                own.start()
                kept.append(own)
            else:
                outs.append(remote(OS.at[1, k], place, to_sib))

    def deliver_on(j):
        staged[j].wait_recv()
        for k in (0, 1):
            place = grad_outs[k].at[:, quarter_of(2)]
            outs.append(remote(SB.at[j - 2, k], place, to_ym if j == 2 else to_ymx))

    @pl.loop(0, 4)
    def _(g):
        rows = pl.ds(pl.multiple_of(g * GROUP, GROUP), GROUP)
        f = FAC[pl.ds(g, 1), :][:, :1]
        CR[rows, :] = (f * dot(S2[0, rows, :], S1[0, rows, :], ((1,), (1,)))).astype(BF)

    to_core, z_hop, z_own, z_sum, y_part = {}, {}, {}, {}, {}

    def cols_of(n):
        return pl.ds(n * CHUNK, CHUNK)

    def half_of(n, h):
        return pl.ds(n * CHUNK + h * (CHUNK // 2), CHUNK // 2)

    def partial(n):
        cols = cols_of(n)

        @pl.loop(0, 2)
        def _(yy):
            rows = pl.ds(pl.multiple_of(yy * 2 * GROUP, 2 * GROUP), 2 * GROUP)
            out = dot(S2[0, rows, :], W[0, cols, :], ((1,), (1,)))
            for cc in (0, 1):
                group = pl.ds(pl.multiple_of((yy * 2 + cc) * GROUP, GROUP), GROUP)
                mine = out[cc * GROUP : (cc + 1) * GROUP]
                mine = mine + dot(CR[group, :], X[0, group, cols], ((1,), (0,)))
                PB[yy, cc, :, :, :, cols] = mine.reshape(4, 2, 32, CHUNK).astype(BF)

        to_core[n] = remote(PB.at[:, 1 - c, :, :, :, cols], PR.at[:, :, :, :, cols], to_sib)

    def over_z(n):
        cols = cols_of(n)
        to_core[n].wait_recv()

        @pl.loop(0, 8)
        def _(i):
            a, b = i // 4, lax.rem(i, 4)
            both = PB[a, c, b, :, :, cols].astype(F32) + PR[a, b, :, :, cols].astype(F32)
            PB[a, c, b, :, :, cols] = both.astype(BF)

        part = lambda zz, h: PB.at[:, c, zz, :, :, half_of(n, h)]
        z_hop[n] = [remote(part(z_far, h), ZH.at[n, h], to_z[h]) for h in (0, 1)]
        z_own[n] = [remote(part(z_down, 0), ZF.at[n, 0, 0], to_z[1]), remote(part(z_up, 1), ZF.at[n, 1, 0], to_z[0])]

    def z_relay(n):
        z_sum[n] = []
        for h, zz in enumerate((z_up, z_down)):
            z_hop[n][h].wait_recv()
            cols = half_of(n, h)
            both = PB[:, c, zz, :, :, cols].astype(F32) + ZH[n, h].astype(F32)
            PB[:, c, zz, :, :, cols] = both.astype(BF)
            z_sum[n].append(remote(PB.at[:, c, zz, :, :, cols], ZF.at[n, h, 1], to_z[h]))

    def over_y(n):
        got(z_own[n])
        got(z_sum[n])
        for h in (0, 1):
            cols = half_of(n, h)
            s = PB[:, c, z, :, :, cols].astype(F32) + ZF[n, h, 0].astype(F32) + ZF[n, h, 1].astype(F32)
            RA[:, :, :, cols] = s.astype(BF)
        y_part[n] = [remote(RA.at[y_of[i][0], y_of[i][1], :, cols_of(n)], YA.at[n, i], to_y[i]) for i in range(3)]

    ig_ym, ig_up, ig_down, ig_far = {}, {}, {}, []

    def ig_send(n, m):
        mine = IG.at[z, ylo if m == 0 else 1 - ylo, :, cols_of(n)]
        ig_up[n, m] = remote(mine, mine, to_z[0])
        ig_down[n, m] = remote(mine, mine, to_z[1])

    def spread_rows(n):
        got(y_part[n])
        s = RA[yhi, ylo, :, cols_of(n)].astype(F32)
        for slot in range(3):
            s += YA[n, slot].astype(F32)
        IG[z, ylo, :, cols_of(n)] = s.astype(BF)
        mine = IG.at[z, ylo, :, cols_of(n)]
        ig_ym[n] = remote(mine, mine, to_ym)
        ig_send(n, 0)

    def spread_other(n):
        ig_ym[n].wait_recv()
        ig_send(n, 1)

    def spread_far(n, m):
        yl = ylo if m == 0 else 1 - ylo
        ig_up[n, m].wait_recv()
        block = IG.at[z_down, yl, :, half_of(n, 0)]
        ig_far.append(remote(block, block, to_z[0]))
        ig_down[n, m].wait_recv()
        block = IG.at[z_up, yl, :, half_of(n, 1)]
        ig_far.append(remote(block, block, to_z[1]))

    partial(0)
    first_hops(2)
    over_z(0)
    partial(1)
    directs(2)
    over_z(1)
    z_relay(0)
    partial(2)
    sums(2)
    over_z(2)
    first_hops(0)
    z_relay(1)
    over_y(0)
    partial(3)
    directs(0)
    over_z(3)
    z_relay(2)
    over_y(1)
    spread_rows(0)
    term(x, 1)
    deliver(2)
    z_relay(3)
    sums(0)
    over_y(2)
    spread_other(0)
    spread_rows(1)
    deliver(3)
    spread_far(0, 0)
    spread_far(0, 1)
    over_y(3)
    spread_other(1)
    spread_rows(2)
    deliver_on(2)
    term(x, 0)
    spread_far(1, 0)
    spread_far(1, 1)
    spread_other(2)
    spread_rows(3)
    deliver_on(3)
    spread_far(2, 0)
    spread_far(2, 1)
    spread_other(3)
    deliver(1)
    deliver(0)
    spread_far(3, 0)
    spread_far(3, 1)
    got(ig_far)
    done = pltpu.make_async_copy(IG, input_out, local.at[2])
    done.start()
    got(outs)
    for own in kept:
        own.wait()
    done.wait()
    for copy in pending:
        copy.wait_send()


def on_device(tokens, cotangent, w_in, w_out):
    grad_scale = 1.0 / math.sqrt(TOKENS)
    any_space = pl.BlockSpec(memory_space=pl.ANY)
    vmem = pltpu.VMEM
    grad_in, grad_out, input_grad = pl.pallas_call(
        kernel,
        out_shape=(
            jax.ShapeDtypeStruct((ROWS, 4 * QUARTER), BF),
            jax.ShapeDtypeStruct((ROWS, 4 * QUARTER), BF),
            jax.ShapeDtypeStruct((4, 2, 32, D), BF),
        ),
        in_specs=[any_space] * 4,
        out_specs=(any_space,) * 3,
        scratch_shapes=[
            vmem((2, 4 * GROUP, D), BF),
            vmem((2, D, QUARTER), BF),
            vmem((2, 4 * GROUP, QUARTER), F32),
            vmem((2, 4 * GROUP, QUARTER), F32),
            vmem((2, 2, 4 * GROUP, GROUP), BF),
            vmem((2, 4 * GROUP, QUARTER), BF),
            vmem((2, 4 * GROUP, QUARTER), BF),
            vmem((2, D, QUARTER), BF),
            vmem((4, 2, ROWS, QUARTER), BF),
            vmem((4, 2, ROWS, QUARTER), BF),
            vmem((4, 2, ROWS, QUARTER), BF),
            vmem((4, 2, ROWS, QUARTER), BF),
            vmem((4 * GROUP, GROUP), BF),
            vmem((2, 2, 4, 2, 32, D), BF),
            vmem((2, 4, 2, 32, D), BF),
            vmem((4, 2, 2, 2, 32, CHUNK // 2), BF),
            vmem((4, 2, 2, 2, 2, 32, CHUNK // 2), BF),
            vmem((2, 2, 32, D), BF),
            vmem((4, 3, 32, CHUNK), BF),
            vmem((4, 2, 32, D), BF),
            vmem((2, 2, ROWS, QUARTER), BF),
            vmem((2, 2, ROWS, QUARTER), BF),
            vmem((8, 128), F32),
            vmem((10, 8, 128), F32),
            vmem((8, 128), F32),
            pltpu.SemaphoreType.DMA((192,)),
            pltpu.SemaphoreType.DMA((192,)),
            pltpu.SemaphoreType.DMA((4,)),
        ],
        compiler_params=pltpu.CompilerParams(
            collective_id=0, has_side_effects=True, vmem_limit_bytes=63 * 2**20
        ),
        cost_estimate=pl.CostEstimate(flops=20 * 10**9, bytes_accessed=40 * 2**20, transcendentals=10**6),
    )(tokens, cotangent, w_in, w_out.T)
    return (
        grad_in.astype(F32) * grad_scale,
        (grad_out.astype(F32) * grad_scale).T,
        input_grad.reshape(GROUP, D),
    )


def solution(mesh):
    return jax.shard_map(
        on_device,
        mesh=mesh,
        in_specs=(P("fsdp", None), P("fsdp", None), P("fsdp", "dp"), P("dp", "fsdp")),
        out_specs=(P("fsdp", "dp"), P("dp", "fsdp"), P("fsdp", None)),
        check_vma=False,
    )
```

```python
import math

import jax
import jax.numpy as jnp
from jax import lax
from jax.experimental import pallas as pl
from jax.experimental.pallas import tpu as pltpu
from jax.sharding import PartitionSpec as P

D = 3072
FF = 12288
TOKENS = 4096
GROUP = 256
ROWS = 192
QUARTER = 384
CHUNK = 1024

RADIUS_SHARE = 0.5
EPSILON = 1e-06
BF = jnp.bfloat16
F32 = jnp.float32
MESH = pl.DeviceIdType.MESH


def dot(a, b, dims):
    return lax.dot_general(a, b, (dims, ((), ())), preferred_element_type=F32)


def gelu_pair(h):
    cdf = 0.5 * (1.0 + lax.erf(h * (1.0 / math.sqrt(2.0))))
    pdf = jnp.exp(-0.5 * h * h) * (1.0 / math.sqrt(2.0 * math.pi))
    return h * cdf, cdf + h * pdf


def kernel(
    tok_ref, cot_ref, win_ref, wout_ref, gin_out, gout_out, input_out,
    X, W, HB, GS, GM, S1, S2, T, HOP, FL, FR, OS, CR, PB, PR, ZH, ZF, RA, YA, IG, ST, SB,
    SQ, SQR, FAC, send, recv, local,
):
    dp, fs = lax.axis_index("dp"), lax.axis_index("fsdp")
    z, ylo = dp // 2, lax.rem(dp, 2)
    yhi, x, c = fs // 8, lax.rem(fs // 2, 4), lax.rem(fs, 2)

    def dev(z, ylo, yhi, x, c):
        return (z * 2 + ylo, yhi * 8 + x * 2 + c)

    right, left, across = lax.rem(x + 1, 4), lax.rem(x + 3, 4), lax.rem(x + 2, 4)
    z_up, z_down, z_far = lax.rem(z + 1, 4), lax.rem(z + 3, 4), lax.rem(z + 2, 4)
    to_sib = dev(z, ylo, yhi, x, 1 - c)
    to_quad = [None, to_sib, dev(z, ylo, 1 - yhi, x, c), dev(z, ylo, 1 - yhi, x, 1 - c)]
    to_right, to_left = dev(z, ylo, yhi, right, c), dev(z, ylo, yhi, left, c)
    to_z = [dev(zz, ylo, yhi, x, c) for zz in (z_up, z_down, z_far)]
    to_yn, to_ym, to_y2 = dev(z, 1 - ylo, 1 - yhi, x, c), dev(z, 1 - ylo, yhi, x, c), to_quad[2]
    to_ynx, to_ymx = dev(z, 1 - ylo, 1 - yhi, x, 1 - c), dev(z, 1 - ylo, yhi, x, 1 - c)
    to_y = [to_ym, to_yn, to_y2]
    y_of = [(yhi, 1 - ylo), (1 - yhi, 1 - ylo), (1 - yhi, ylo)]
    z_of = [z_up, z_down, z_far]

    count = [0]
    pending = []

    def remote(src, dst, target, keep=True):
        i = count[0]
        count[0] += 1
        copy = pltpu.make_async_remote_copy(
            src_ref=src, dst_ref=dst, send_sem=send.at[i], recv_sem=recv.at[i],
            device_id=target, device_id_type=MESH,
        )
        copy.start()
        if keep:
            pending.append(copy)
        return copy

    member = [(yhi, c), (yhi, 1 - c), (1 - yhi, c), (1 - yhi, 1 - c)]

    def rows_of(xx, j):
        yy, cc = member[j]
        return pl.ds(pl.multiple_of((yy * 8 + xx * 2 + cc) * ROWS, 64), ROWS)

    def quarter_of(j):
        yy, cc = member[j]
        return pl.ds(pl.multiple_of((yy * 2 + cc) * QUARTER, 128), QUARTER)

    def group_rows(j, start=0, size=GROUP):
        yy, cc = member[j]
        return pl.ds(pl.multiple_of((yy * 2 + cc) * GROUP + start, 32), size)

    barrier = pltpu.get_barrier_semaphore()
    peers = [to_sib, to_quad[2], to_quad[3], to_right, to_left, *to_z, to_yn, to_ym, to_ynx, to_ymx]
    tokens_of, weights_of = (tok_ref, cot_ref), (win_ref, wout_ref)
    copies = [
        pltpu.make_async_copy(weights_of[k].at[:, quarter_of(0)], W.at[k, rows_of(x, 0)], local.at[k])
        for k in (0, 1)
    ] + [pltpu.make_async_copy(tokens_of[k], X.at[k, group_rows(0)], local.at[2 + k]) for k in (0, 1)]
    for copy in copies:
        copy.start()
    for peer in peers:
        pl.semaphore_signal(barrier, inc=1, device_id=peer, device_id_type=MESH)
    pl.semaphore_wait(barrier, len(peers))

    quad = [None] * 4

    def to_member(j):
        quad[j] = [
            remote(weights_of[k].at[:, quarter_of(j)], W.at[k, rows_of(x, 0)], to_quad[j]) for k in (0, 1)
        ]

    def to_partner(k):
        rows = pl.ds(pl.multiple_of(z * 64 + ylo * 32, 32), 32)
        return remote(tokens_of[k].at[rows], X.at[k, group_rows(0, z * 64 + ylo * 32, 32)], to_yn)

    tok_n = [to_partner(k) for k in (0, 1)]
    stage = {
        j: [remote(weights_of[k].at[:, quarter_of(j)], ST.at[j - 2, k], to_ym) for k in (0, 1)] for j in (2, 3)
    }
    to_member(1)

    def stage_on(j):
        for copy in stage[j]:
            copy.wait_recv()
        quad[j] = [remote(ST.at[j - 2], W.at[:, rows_of(x, 0)], to_yn if j == 2 else to_ynx)]

    from_left, from_right = [None] * 4, [None] * 4

    def ring(j):
        block = W.at[:, rows_of(x, j)]
        from_left[j] = remote(block, block, to_right)
        from_right[j] = remote(block, block, to_left)

    def relay_right(j):
        from_left[j].wait_recv()
        block = W.at[:, rows_of(left, j)]
        return remote(block, block, to_right)

    def relay_left(j):
        from_right[j].wait_recv()
        block = W.at[:, rows_of(right, j)]
        return remote(block, block, to_left)

    for copy in copies[:2]:
        copy.wait()
    ring(0)
    for copy in copies[2:]:
        copy.wait()
    tok_c = [remote(X.at[k, group_rows(0)], X.at[k, group_rows(0)], to_sib) for k in (0, 1)]

    def got(copies):
        for copy in copies:
            copy.wait_recv()

    def gram_of(j):
        @pl.loop(0, 2)
        def _(k):
            rows = group_rows(j)
            block = X[k, rows, :]
            g = dot(block, block, ((1,), (1,)))
            hi = g.astype(BF)
            GM[k, 0, rows, :] = hi
            GM[k, 1, rows, :] = (g - hi.astype(F32)).astype(BF)

    def hidden(yy, xx, half, first=False, both=False):
        base = pl.ds(pl.multiple_of((half * 4 + xx) * QUARTER, 128), QUARTER)
        rows = pl.ds(pl.multiple_of(yy * 2 * GROUP, 2 * GROUP), 2 * GROUP)

        @pl.loop(0, 2)
        def _(k):
            out = dot(X[k, rows, base], W[k, base, :], ((1,), (0,)))
            if both:
                rest = pl.ds(pl.multiple_of((4 + xx) * QUARTER, 128), QUARTER)
                out = out + dot(X[k, rows, rest], W[k, rest, :], ((1,), (0,)))
            if not first:
                out = out + HB[k, rows, :]
            HB[k, rows, :] = out

    part_rows = lambda zz, yl: group_rows(2, zz * 64 + yl * 32, 32)
    fwd = []
    up, down, far = {}, {}, {}

    def forward(k, zz, yl):
        block = X.at[k, part_rows(zz, yl)]
        fwd.append(remote(block, block, to_sib))

    def spread(k, n):
        yl = 1 - ylo if n == 0 else ylo
        block = X.at[k, part_rows(z, yl)]
        up[k, n] = remote(block, block, to_z[0])
        down[k, n] = remote(block, block, to_z[1])
        forward(k, z, yl)

    def pass_on(k, n):
        yl = 1 - ylo if n == 0 else ylo
        if k == 0:
            up[k, n].wait_recv()
            block = X.at[k, part_rows(z_down, yl)]
            far[k, n] = remote(block, block, to_z[0])
            forward(k, z_down, yl)
        else:
            down[k, n].wait_recv()
            block = X.at[k, part_rows(z_up, yl)]
            far[k, n] = remote(block, block, to_z[1])
            forward(k, z_up, yl)

    def rest(k, n):
        yl = 1 - ylo if n == 0 else ylo
        if k == 0:
            down[k, n].wait_recv()
            forward(k, z_up, yl)
        else:
            up[k, n].wait_recv()
            forward(k, z_down, yl)

    def last(k, n):
        yl = 1 - ylo if n == 0 else ylo
        far[k, n].wait_recv()
        forward(k, z_far, yl)

    tok_m = [None] * 2

    def from_partner(k):
        tok_n[k].wait_recv()
        block = X.at[k, part_rows(z, 1 - ylo)]
        tok_m[k] = remote(block, block, to_ym)
        spread(k, 0)

    other = 1 - yhi
    got(quad[1])
    ring(1)
    from_partner(0)
    gram_of(0)
    relays = [relay_right(0)]
    stage_on(2)
    from_partner(1)
    pass_on(0, 0)
    relays += [relay_left(1)]
    stage_on(3)
    rest(0, 0)
    pass_on(1, 0)
    got(tok_c)
    gram_of(1)
    got(quad[2])
    ring(2)
    tok_m[0].wait_recv()
    spread(0, 1)
    rest(1, 0)
    hidden(yhi, x, yhi, first=True)
    tok_m[1].wait_recv()
    spread(1, 1)
    last(0, 0)
    last(1, 0)
    got(quad[3])
    ring(3)
    got([from_left[1], from_right[0]])
    hidden(yhi, left, yhi)
    pass_on(0, 1)
    hidden(yhi, right, yhi)
    got(relays)
    hidden(yhi, across, yhi)
    pass_on(1, 1)
    rest(0, 1)
    rest(1, 1)
    hidden(yhi, x, other)
    late = [relay_right(2), relay_left(3)]
    last(0, 1)
    last(1, 1)
    got([from_left[3], from_right[2]])
    hidden(yhi, left, other)
    hidden(yhi, right, other)
    got(fwd)
    gram_of(2)
    gram_of(3)
    hidden(other, x, 0, first=True, both=True)
    hidden(other, left, 0, both=True)
    hidden(other, right, 0, both=True)
    hidden(other, across, yhi)
    got(late)
    hidden(yhi, across, other)
    hidden(other, across, other)

    SQ[...] = jnp.zeros_like(SQ)

    @pl.loop(0, 4)
    def _(g):
        rows = pl.ds(pl.multiple_of(g * GROUP, GROUP), GROUP)

        @pl.loop(0, 4)
        def _(s):
            part = pl.ds(pl.multiple_of(g * GROUP + s * 64, 64), 64)
            act, der = gelu_pair(HB[0, part, :])
            S1[0, part, :] = (HB[1, part, :] * der).astype(BF)
            S1[1, part, :] = act.astype(BF)

        @pl.loop(0, 2)
        def _(k):
            s = S1[k, rows, :]
            gs = dot(GM[k, 0, rows, :], s, ((1,), (0,))) + dot(GM[k, 1, rows, :], s, ((1,), (0,)))
            GS[k, rows, :] = gs
            row = jnp.sum(gs * s.astype(F32), axis=0, keepdims=True)
            row = row[:, :128] + row[:, 128:256] + row[:, 256:]
            SQ[pl.ds(g, 1), :] += row

    def exchange(slot, targets):
        sums = [remote(SQ, SQR.at[slot + i], t, keep=False) for i, t in enumerate(targets)]
        for copy in sums:
            copy.wait_recv()
            copy.wait_send()
        total = SQ[...]
        for i in range(len(targets)):
            total += SQR[slot + i]
        SQ[...] = total

    exchange(0, [to_sib, *to_y, to_quad[3], to_ynx, to_ymx])
    exchange(7, to_z)
    square = jnp.sum(SQ[...], axis=1, keepdims=True)
    FAC[...] = jnp.broadcast_to(RADIUS_SHARE * math.sqrt(D + FF) / jnp.sqrt(square + EPSILON), FAC.shape)

    @pl.loop(0, 16)
    def _(s):
        part = pl.ds(pl.multiple_of(s * 64, 64), 64)
        f = FAC[pl.ds(s // 4, 1), :][:, :1]
        act, der = gelu_pair(HB[0, part, :] + f * GS[0, part, :])
        S2[0, part, :] = ((HB[1, part, :] + f * GS[1, part, :]) * der).astype(BF)
        S2[1, part, :] = act.astype(BF)

    def term(xx, dy):
        yy = yhi if dy == 0 else 1 - yhi
        base = pl.ds(pl.multiple_of((yy * 4 + xx) * QUARTER, 128), QUARTER)

        @pl.loop(0, 2)
        def _(k):
            T[k, base, :] = dot(X[k, :, base], S2[k], ((0,), (0,))).astype(BF)

    def send_term(src_x, j, dst, target):
        return remote(T.at[:, rows_of(src_x, j)], dst, target)

    hop, final_left, final_right = [None] * 4, [None] * 4, [None] * 4

    def add_hop(xx, j):
        hop[j].wait_recv()
        rows = rows_of(xx, j)
        T[:, rows, :] = (T[:, rows, :].astype(F32) + HOP[j].astype(F32)).astype(BF)

    def first_hops(j):
        term(across, j // 2)
        hop[j] = send_term(across, j, HOP.at[j], to_right)
        hop[j + 1] = send_term(across, j + 1, HOP.at[j + 1], to_left)

    def directs(j):
        term(right, j // 2)
        final_left[j + 1] = send_term(right, j + 1, FL.at[j + 1], to_right)
        term(left, j // 2)
        final_right[j] = send_term(left, j, FR.at[j], to_left)

    def sums(j):
        add_hop(right, j)
        final_left[j] = send_term(right, j, FL.at[j], to_right)
        add_hop(left, j + 1)
        final_right[j + 1] = send_term(left, j + 1, FR.at[j + 1], to_left)

    def total(j):
        final_left[j].wait_recv()
        final_right[j].wait_recv()
        OS[j] = (T[:, rows_of(x, j), :].astype(F32) + FL[j].astype(F32) + FR[j].astype(F32)).astype(BF)

    outs, kept, staged = [], [], {}
    grad_outs = (gin_out, gout_out)

    def deliver(j):
        total(j)
        if j >= 2:
            staged[j] = remote(OS.at[j], SB.at[j - 2], to_yn)
            return
        for k in (0, 1):
            place = grad_outs[k].at[:, quarter_of(0)]
            if j == 0:
                own = pltpu.make_async_copy(OS.at[0, k], place, local.at[k])
                own.start()
                kept.append(own)
            else:
                outs.append(remote(OS.at[1, k], place, to_sib))

    def deliver_on(j):
        staged[j].wait_recv()
        for k in (0, 1):
            place = grad_outs[k].at[:, quarter_of(2)]
            outs.append(remote(SB.at[j - 2, k], place, to_ym if j == 2 else to_ymx))

    @pl.loop(0, 4)
    def _(g):
        rows = pl.ds(pl.multiple_of(g * GROUP, GROUP), GROUP)
        f = FAC[pl.ds(g, 1), :][:, :1]
        CR[rows, :] = (f * dot(S2[0, rows, :], S1[0, rows, :], ((1,), (1,)))).astype(BF)

    to_core, z_hop, z_own, z_sum, y_part = {}, {}, {}, {}, {}

    def cols_of(n):
        return pl.ds(n * CHUNK, CHUNK)

    def half_of(n, h):
        return pl.ds(n * CHUNK + h * (CHUNK // 2), CHUNK // 2)

    def partial(n):
        cols = cols_of(n)

        @pl.loop(0, 2)
        def _(yy):
            rows = pl.ds(pl.multiple_of(yy * 2 * GROUP, 2 * GROUP), 2 * GROUP)
            out = dot(S2[0, rows, :], W[0, cols, :], ((1,), (1,)))
            for cc in (0, 1):
                group = pl.ds(pl.multiple_of((yy * 2 + cc) * GROUP, GROUP), GROUP)
                mine = out[cc * GROUP : (cc + 1) * GROUP]
                mine = mine + dot(CR[group, :], X[0, group, cols], ((1,), (0,)))
                PB[yy, cc, :, :, :, cols] = mine.reshape(4, 2, 32, CHUNK).astype(BF)

        to_core[n] = remote(PB.at[:, 1 - c, :, :, :, cols], PR.at[:, :, :, :, cols], to_sib)

    def over_z(n):
        cols = cols_of(n)
        to_core[n].wait_recv()

        @pl.loop(0, 8)
        def _(i):
            a, b = i // 4, lax.rem(i, 4)
            both = PB[a, c, b, :, :, cols].astype(F32) + PR[a, b, :, :, cols].astype(F32)
            PB[a, c, b, :, :, cols] = both.astype(BF)

        part = lambda zz, h: PB.at[:, c, zz, :, :, half_of(n, h)]
        z_hop[n] = [remote(part(z_far, h), ZH.at[n, h], to_z[h]) for h in (0, 1)]
        z_own[n] = [remote(part(z_down, 0), ZF.at[n, 0, 0], to_z[1]), remote(part(z_up, 1), ZF.at[n, 1, 0], to_z[0])]

    def z_relay(n):
        z_sum[n] = []
        for h, zz in enumerate((z_up, z_down)):
            z_hop[n][h].wait_recv()
            cols = half_of(n, h)
            both = PB[:, c, zz, :, :, cols].astype(F32) + ZH[n, h].astype(F32)
            PB[:, c, zz, :, :, cols] = both.astype(BF)
            z_sum[n].append(remote(PB.at[:, c, zz, :, :, cols], ZF.at[n, h, 1], to_z[h]))

    def over_y(n):
        got(z_own[n])
        got(z_sum[n])
        for h in (0, 1):
            cols = half_of(n, h)
            s = PB[:, c, z, :, :, cols].astype(F32) + ZF[n, h, 0].astype(F32) + ZF[n, h, 1].astype(F32)
            RA[:, :, :, cols] = s.astype(BF)
        y_part[n] = [remote(RA.at[y_of[i][0], y_of[i][1], :, cols_of(n)], YA.at[n, i], to_y[i]) for i in range(3)]

    ig_ym, ig_up, ig_down, ig_far = {}, {}, {}, []

    def ig_send(n, m):
        mine = IG.at[z, ylo if m == 0 else 1 - ylo, :, cols_of(n)]
        ig_up[n, m] = remote(mine, mine, to_z[0])
        ig_down[n, m] = remote(mine, mine, to_z[1])

    def spread_rows(n):
        got(y_part[n])
        s = RA[yhi, ylo, :, cols_of(n)].astype(F32)
        for slot in range(3):
            s += YA[n, slot].astype(F32)
        IG[z, ylo, :, cols_of(n)] = s.astype(BF)
        mine = IG.at[z, ylo, :, cols_of(n)]
        ig_ym[n] = remote(mine, mine, to_ym)
        ig_send(n, 0)

    def spread_other(n):
        ig_ym[n].wait_recv()
        ig_send(n, 1)

    def spread_far(n, m):
        yl = ylo if m == 0 else 1 - ylo
        ig_up[n, m].wait_recv()
        block = IG.at[z_down, yl, :, half_of(n, 0)]
        ig_far.append(remote(block, block, to_z[0]))
        ig_down[n, m].wait_recv()
        block = IG.at[z_up, yl, :, half_of(n, 1)]
        ig_far.append(remote(block, block, to_z[1]))

    partial(0)
    first_hops(2)
    over_z(0)
    partial(1)
    directs(2)
    over_z(1)
    z_relay(0)
    sums(2)
    partial(2)
    over_z(2)
    first_hops(0)
    z_relay(1)
    over_y(0)
    directs(0)
    z_relay(2)
    over_y(1)
    spread_rows(0)
    term(x, 1)
    deliver(2)
    sums(0)
    over_y(2)
    spread_other(0)
    spread_rows(1)
    deliver(3)
    spread_far(0, 0)
    spread_far(0, 1)
    spread_other(1)
    spread_rows(2)
    deliver_on(2)
    term(x, 0)
    spread_far(1, 0)
    spread_far(1, 1)
    deliver_on(3)
    spread_other(2)
    deliver(1)
    deliver(0)
    spread_far(2, 0)
    spread_far(2, 1)
    got(ig_far)
    done = pltpu.make_async_copy(IG, input_out, local.at[2])
    done.start()
    got(outs)
    for own in kept:
        own.wait()
    done.wait()
    for copy in pending:
        copy.wait_send()


def on_device(tokens, cotangent, w_in, w_out):
    grad_scale = 1.0 / math.sqrt(TOKENS)
    any_space = pl.BlockSpec(memory_space=pl.ANY)
    vmem = pltpu.VMEM
    grad_in, grad_out, input_grad = pl.pallas_call(
        kernel,
        out_shape=(
            jax.ShapeDtypeStruct((ROWS, 4 * QUARTER), BF),
            jax.ShapeDtypeStruct((ROWS, 4 * QUARTER), BF),
            jax.ShapeDtypeStruct((4, 2, 32, D), BF),
        ),
        in_specs=[any_space] * 4,
        out_specs=(any_space,) * 3,
        scratch_shapes=[
            vmem((2, 4 * GROUP, D), BF),
            vmem((2, D, QUARTER), BF),
            vmem((2, 4 * GROUP, QUARTER), F32),
            vmem((2, 4 * GROUP, QUARTER), F32),
            vmem((2, 2, 4 * GROUP, GROUP), BF),
            vmem((2, 4 * GROUP, QUARTER), BF),
            vmem((2, 4 * GROUP, QUARTER), BF),
            vmem((2, D, QUARTER), BF),
            vmem((4, 2, ROWS, QUARTER), BF),
            vmem((4, 2, ROWS, QUARTER), BF),
            vmem((4, 2, ROWS, QUARTER), BF),
            vmem((4, 2, ROWS, QUARTER), BF),
            vmem((4 * GROUP, GROUP), BF),
            vmem((2, 2, 4, 2, 32, D), BF),
            vmem((2, 4, 2, 32, D), BF),
            vmem((3, 2, 2, 2, 32, CHUNK // 2), BF),
            vmem((3, 2, 2, 2, 2, 32, CHUNK // 2), BF),
            vmem((2, 2, 32, D), BF),
            vmem((3, 3, 32, CHUNK), BF),
            vmem((4, 2, 32, D), BF),
            vmem((2, 2, ROWS, QUARTER), BF),
            vmem((2, 2, ROWS, QUARTER), BF),
            vmem((8, 128), F32),
            vmem((10, 8, 128), F32),
            vmem((8, 128), F32),
            pltpu.SemaphoreType.DMA((192,)),
            pltpu.SemaphoreType.DMA((192,)),
            pltpu.SemaphoreType.DMA((4,)),
        ],
        compiler_params=pltpu.CompilerParams(
            collective_id=0, has_side_effects=True, vmem_limit_bytes=63 * 2**20
        ),
        cost_estimate=pl.CostEstimate(flops=20 * 10**9, bytes_accessed=40 * 2**20, transcendentals=10**6),
    )(tokens, cotangent, w_in, w_out.T)
    return (
        grad_in.astype(F32) * grad_scale,
        (grad_out.astype(F32) * grad_scale).T,
        input_grad.reshape(GROUP, D),
    )


def solution(mesh):
    return jax.shard_map(
        on_device,
        mesh=mesh,
        in_specs=(P("fsdp", None), P("fsdp", None), P("fsdp", "dp"), P("dp", "fsdp")),
        out_specs=(P("fsdp", "dp"), P("dp", "fsdp"), P("fsdp", None)),
        check_vma=False,
    )
```
